512 devices in a mesh: dp: 4 (over z_hi), tm: 4 (over x), space: 32 (over z_lo, y, core).
Axes of the slice: x: 4, y: 4, z: 16 (z_hi: 4, z_lo: 4; z = z_hi * 4 + z_lo), core: 2. Of those that a mesh axis runs over, the one named last changes fastest.
Arguments:
- q_spatial: bfloat16 [4, 8, 2048, 1152], P('dp', 'tm', 'space'), may hold values from -6 to 6
- k_spatial: bfloat16 [4, 8, 2048, 1152], P('dp', 'tm', 'space'), may hold values from -6 to 6
- v_spatial: bfloat16 [4, 8, 2048, 1152], P('dp', 'tm', 'space'), may hold values from -6 to 6
- grad_spatial: bfloat16 [4, 8, 2048, 1152], P('dp', 'tm', 'space'), may hold values from -6 to 6
- q_temporal: bfloat16 [4, 8, 2048, 1152], P('dp', 'tm', 'space'), may hold values from -6 to 6
- k_temporal: bfloat16 [4, 8, 2048, 1152], P('dp', 'tm', 'space'), may hold values from -6 to 6
- v_temporal: bfloat16 [4, 8, 2048, 1152], P('dp', 'tm', 'space'), may hold values from -6 to 6
- grad_out: bfloat16 [4, 8, 2048, 1152], P('dp', 'tm', 'space'), may hold values from -6 to 6
- w_tout: bfloat16 [1152, 1152], P('dp', 'tm'), may hold values from -0.1875 to 0.1875
Outputs:
- dq_spatial: bfloat16 [4, 8, 2048, 1152], P('dp', 'tm', 'space')
- dk_spatial: bfloat16 [4, 8, 2048, 1152], P('dp', 'tm', 'space')
- dv_spatial: bfloat16 [4, 8, 2048, 1152], P('dp', 'tm', 'space')
- dq_temporal: bfloat16 [4, 8, 2048, 1152], P('dp', 'tm', 'space')
- dk_temporal: bfloat16 [4, 8, 2048, 1152], P('dp', 'tm', 'space')
- dv_temporal: bfloat16 [4, 8, 2048, 1152], P('dp', 'tm', 'space')
- d_w_tout: float32 [1152, 1152], P('dp', 'tm')
The draws below stay inside these ranges and needn't reach their ends.
All inputs are finite; a program needn't handle non-finite values.
Results may differ from the reference program's by a relative error of at most 0.015.
Values may be sent and summed in bfloat16 or wider, within the bound.
No kernel may reach another device: no remote copies, remote signals or barrier semaphores. Data moves between devices by JAX's collectives and lax.ppermute only.
A program may use at most 64 MiB of HBM per device.

```python
import math
import jax
import jax.numpy as jnp
from jax import lax

D = 1152
HEADS = 16
HDIM = 72
CLIPS = 4
FRAMES = 8
S = 2048


def draw_q_spatial(key, part):
    key = jax.random.fold_in(key, 1)
    extent = (CLIPS, FRAMES, S, D)
    field = jax.random.truncated_normal(key, -6.0, 6.0, extent, jnp.float32)
    return field.astype(jnp.bfloat16)


def draw_k_spatial(key, part):
    key = jax.random.fold_in(key, 2)
    extent = (CLIPS, FRAMES, S, D)
    field = jax.random.truncated_normal(key, -6.0, 6.0, extent, jnp.float32)
    return field.astype(jnp.bfloat16)


def draw_q_temporal(key, part):
    key = jax.random.fold_in(key, 3)
    extent = (CLIPS, FRAMES, S, D)
    field = jax.random.truncated_normal(key, -6.0, 6.0, extent, jnp.float32)
    return field.astype(jnp.bfloat16)


def draw_k_temporal(key, part):
    key = jax.random.fold_in(key, 4)
    extent = (CLIPS, FRAMES, S, D)
    field = jax.random.truncated_normal(key, -6.0, 6.0, extent, jnp.float32)
    return field.astype(jnp.bfloat16)


def level_of(rng, shape, pieces, least, high):
    def one(axis_at, parts):
        draws = jax.random.uniform(jax.random.fold_in(jax.random.fold_in(rng, 6), axis_at), (parts,), jnp.float32, least / len(pieces), high / len(pieces))
        return jnp.repeat(jnp.exp(draws), shape[axis_at] // parts).reshape((-1,) + (1,) * (len(shape) - axis_at - 1))

    factor_of = one(*pieces[0])
    for cut in pieces[1:]:
        factor_of = factor_of * one(*cut)
    return factor_of


def scatter_about(own_key, shape, deviation, limit, shards=(), kind=jnp.bfloat16):
    entries = deviation * jax.random.normal(own_key, shape, jnp.float32)
    if shards:
        entries = entries * level_of(own_key, shape, shards, -0.22, 0.18)
    return jnp.clip(entries, -limit, limit).astype(kind)


def setup_inputs(seed: int = 0) -> dict:
    streams_of = jax.random.split(jax.random.key(seed), 10)
    q_spatial = draw_q_spatial(jax.random.fold_in(streams_of[9], 71), 0)
    k_spatial = draw_k_spatial(jax.random.fold_in(streams_of[9], 71), 0)
    v_spatial = scatter_about(streams_of[2], (CLIPS, FRAMES, S, D), 1.0, 6.0, ((0, 4), (1, 4), (2, 32)))
    grad_spatial = scatter_about(streams_of[3], (CLIPS, FRAMES, S, D), 1.0, 6.0, ((0, 4), (1, 4), (2, 32)))
    q_temporal = draw_q_temporal(jax.random.fold_in(streams_of[9], 71), 0)
    k_temporal = draw_k_temporal(jax.random.fold_in(streams_of[9], 71), 0)
    v_temporal = scatter_about(streams_of[6], (CLIPS, FRAMES, S, D), 1.0, 6.0, ((0, 4), (1, 4), (2, 32)))
    grad_out = scatter_about(streams_of[7], (CLIPS, FRAMES, S, D), 1.0, 6.0, ((0, 4), (1, 4), (2, 32)))
    w_tout = scatter_about(streams_of[8], (D, D), D ** -0.5, 0.1875, ((0, 4), (1, 4)))
    return dict(q_spatial=q_spatial, k_spatial=k_spatial, v_spatial=v_spatial, grad_spatial=grad_spatial, q_temporal=q_temporal, k_temporal=k_temporal, v_temporal=v_temporal, grad_out=grad_out, w_tout=w_tout)


def attend_back(queries, keys_in, values, out_grad):
    scale = 1.0 / math.sqrt(queries.shape[-1])
    query_f = queries.astype(jnp.float32)
    key_f = keys_in.astype(jnp.float32)
    value_f = values.astype(jnp.float32)
    grad_f = out_grad.astype(jnp.float32)
    scores = jnp.einsum('...id,...jd->...ij', query_f, key_f) * scale
    peak = lax.optimization_barrier(jnp.max(scores, axis=-1, keepdims=True))
    raised = jnp.exp(scores - peak)
    weights = raised / lax.optimization_barrier(jnp.sum(raised, axis=-1, keepdims=True))
    prob_grad = jnp.einsum('...id,...jd->...ij', grad_f, value_f)
    inner = lax.optimization_barrier(jnp.sum(weights * prob_grad, axis=-1, keepdims=True))
    score_low = lax.optimization_barrier((weights * (prob_grad - inner)).astype(jnp.bfloat16)).astype(jnp.float32)
    weight_low = lax.optimization_barrier(weights.astype(jnp.bfloat16)).astype(jnp.float32)
    query_grad = jnp.einsum('...ij,...jd->...id', score_low, key_f) * scale
    key_grad = jnp.einsum('...ij,...id->...jd', score_low, query_f) * scale
    value_grad = jnp.einsum('...ij,...id->...jd', weight_low, grad_f)
    output = jnp.einsum('...ij,...jd->...id', weight_low, value_f)
    return (query_grad.astype(jnp.bfloat16), key_grad.astype(jnp.bfloat16), value_grad.astype(jnp.bfloat16), output.astype(jnp.bfloat16))

def split_heads(field):
    return field.reshape(CLIPS, FRAMES, S, HEADS, HDIM)

def spatial_items(field):
    return split_heads(field).transpose(0, 1, 3, 2, 4).reshape(CLIPS * FRAMES * HEADS, S, HDIM)

def spatial_join(field):
    return field.reshape(CLIPS, FRAMES, HEADS, S, HDIM).transpose(0, 1, 3, 2, 4).reshape(CLIPS, FRAMES, S, D)

def temporal_items(field):
    return split_heads(field).transpose(0, 2, 3, 1, 4)

def temporal_join(field):
    return field.transpose(0, 3, 1, 2, 4).reshape(CLIPS, FRAMES, S, D)

def spatial_one(group):
    results = attend_back(group[0], group[1], group[2], group[3])
    return (results[0], results[1], results[2])

def reference(q_spatial, k_spatial, v_spatial, grad_spatial, q_temporal, k_temporal, v_temporal, grad_out, w_tout):
    spatial = lax.map(spatial_one, (spatial_items(q_spatial), spatial_items(k_spatial), spatial_items(v_spatial), spatial_items(grad_spatial)))
    grad_rows = grad_out.reshape(CLIPS * FRAMES * S, D)
    temporal_grad = jnp.dot(grad_rows, w_tout, preferred_element_type=jnp.float32).astype(jnp.bfloat16)
    temporal_grad = temporal_grad.reshape(CLIPS, FRAMES, S, D)
    results = attend_back(temporal_items(q_temporal), temporal_items(k_temporal), temporal_items(v_temporal), temporal_items(temporal_grad))
    output_rows = temporal_join(results[3]).reshape(CLIPS * FRAMES * S, D)
    weight_scale = 1.0 / math.sqrt(CLIPS * FRAMES * S)
    weight_grad = jnp.dot(grad_rows.T, output_rows, preferred_element_type=jnp.float32) * weight_scale
    return (spatial_join(spatial[0]), spatial_join(spatial[1]), spatial_join(spatial[2]), temporal_join(results[0]), temporal_join(results[1]), temporal_join(results[2]), weight_grad)
```

```python
import math
import functools
import jax
import jax.numpy as jnp
from jax import lax
from jax.experimental import pallas as pl
from jax.experimental.pallas import tpu as pltpu
from jax.sharding import PartitionSpec as P

HEADS = 16
HDIM = 72
LANES = 128
HALF = 64
FOLD = 40
F32 = jnp.float32
BF16 = jnp.bfloat16
LIMIT = 56 * 1024 * 1024
LAST = (((1,), (1,)), ((), ()))


def vmem_specs(count):
    return [pl.BlockSpec(memory_space=pltpu.VMEM)] * count


def low_lanes(rows):
    return lax.broadcasted_iota(jnp.int32, (rows, LANES), 1) < HALF


def swap(block):
    return pltpu.roll(block, HALF, 1)


def pack_kernel(q_ref, k_ref, v_ref, g_ref, out_ref):
    for frame in range(2):
        for pair, (first, second) in enumerate(((q_ref, k_ref), (v_ref, g_ref))):
            rows = jnp.concatenate([first[frame], second[frame]], axis=0).astype(F32)
            columns = rows.T
            for head in range(HEADS):
                out_ref[frame * HEADS + head, pair] = columns[
                    head * HDIM : (head + 1) * HDIM
                ].astype(BF16)


def pack(q, k, v, g):
    return pl.pallas_call(
        pack_kernel,
        out_shape=jax.ShapeDtypeStruct((2 * HEADS, 2, HDIM, LANES), BF16),
        in_specs=vmem_specs(4),
        out_specs=pl.BlockSpec(memory_space=pltpu.VMEM),
        compiler_params=pltpu.CompilerParams(vmem_limit_bytes=LIMIT),
        name="spatial_pack",
    )(q, k, v, g)


def attend_kernel(
    in_ref, out_ref, q_t, k_t, g_t, q_n, k_n, v_n, g_n, s_buf, p_buf, dq_t, dk_n, dv_n, *, step
):
    length = q_t.shape[1]
    pairs = length // LANES
    scale = 1.0 / math.sqrt(HDIM)
    power = scale * math.log2(math.e)

    def split(j, pair):
        first = in_ref[2 * j, pair].astype(F32)
        second = in_ref[2 * j + 1, pair].astype(F32)
        low = low_lanes(HDIM)
        return (
            jnp.where(low, first, swap(second)),
            jnp.where(low, swap(first), second),
        )

    for j in range(pairs):
        at = slice(j * LANES, (j + 1) * LANES)
        q, k = split(j, 0)
        v, g = split(j, 1)
        q_t[:, at] = q.astype(BF16)
        k_t[:, at] = k.astype(BF16)
        g_t[:, at] = g.astype(BF16)
        q_n[at, :] = q.T.astype(BF16)
        k_n[at, :] = k.T.astype(BF16)
        v_n[at, :] = v.T.astype(BF16)
        g_n[at, :] = g.T.astype(BF16)

    blocks = length // step

    def products(i, slot):
        at = pl.ds(pl.multiple_of(i * step, step), step)
        s_buf[slot] = jnp.dot(k_n[...], q_t[:, at], preferred_element_type=F32)
        p_buf[slot] = jnp.dot(v_n[...], g_t[:, at], preferred_element_type=F32)

    def rest(i, slot, first):
        at = pl.ds(pl.multiple_of(i * step, step), step)
        scores = s_buf[slot]
        peak = jnp.max(scores, axis=0, keepdims=True)
        raised = jnp.exp2((scores - peak) * power)
        over = 1.0 / jnp.sum(raised, axis=0, keepdims=True)
        grads = p_buf[slot]
        inner = jnp.sum(raised * grads, axis=0, keepdims=True) * over
        weights = raised * over
        low_w = weights.astype(BF16)
        low_s = (weights * (grads - inner)).astype(BF16)
        dv = jnp.dot(low_w, g_n[at, :], preferred_element_type=F32)
        dk = jnp.dot(low_s, q_n[at, :], preferred_element_type=F32)
        if first:
            dv_n[...] = dv
            dk_n[...] = dk
        else:
            dv_n[...] += dv
            dk_n[...] += dk
        dq_t[:, at] = jnp.dot(k_t[...], low_s, preferred_element_type=F32) * scale

    products(0, 0)
    products(1, 1)
    rest(0, 0, True)

    def body(i, _):
        slot = lax.rem(i, 2)
        products(i + 1, 1 - slot)
        rest(i, slot, False)
        return 0

    lax.fori_loop(1, blocks - 1, body, 0)
    rest(blocks - 1, (blocks - 1) % 2, False)

    for j in range(pairs):
        at = slice(j * LANES, (j + 1) * LANES)
        dq = dq_t[:, at]
        dk = (dk_n[at, :] * scale).T
        dv = dv_n[at, :].T
        low = low_lanes(HDIM)
        low_f = low_lanes(FOLD)
        upper, lower = dv[:FOLD], dv[HDIM - FOLD :]
        out_ref[2 * j] = jnp.concatenate(
            [jnp.where(low, dq, swap(dk)), jnp.where(low_f, upper, swap(lower))], axis=0
        ).astype(BF16)
        out_ref[2 * j + 1] = jnp.concatenate(
            [jnp.where(low, swap(dq), dk), jnp.where(low_f, swap(upper), lower)], axis=0
        ).astype(BF16)


def attend(received, step=256):
    sources = received.shape[0]
    length = sources * HALF
    wide = pltpu.VMEM((HDIM, length), BF16)
    tall = pltpu.VMEM((length, HDIM), BF16)
    return pl.pallas_call(
        functools.partial(attend_kernel, step=step),
        out_shape=jax.ShapeDtypeStruct((sources, HDIM + FOLD, LANES), BF16),
        in_specs=vmem_specs(1),
        out_specs=pl.BlockSpec(memory_space=pltpu.VMEM),
        scratch_shapes=[
            wide, wide, wide, tall, tall, tall, tall,
            pltpu.VMEM((2, length, step), F32),
            pltpu.VMEM((2, length, step), F32),
            pltpu.VMEM((HDIM, length), F32),
            pltpu.VMEM((length, HDIM), F32),
            pltpu.VMEM((length, HDIM), F32),
        ],
        compiler_params=pltpu.CompilerParams(vmem_limit_bytes=LIMIT),
        cost_estimate=pl.CostEstimate(
            flops=10 * length * length * 256, bytes_accessed=2200000, transcendentals=length * length
        ),
        name="spatial_attention",
    )(received)


def unpack_kernel(in_ref, dq_ref, dk_ref, dv_ref):
    low = low_lanes(HEADS * HDIM)
    values = []
    for frame in range(2):
        items = [in_ref[frame * HEADS + head].astype(F32) for head in range(HEADS)]
        both = jnp.concatenate([item[:HDIM] for item in items], axis=0).T.astype(BF16)
        dq_ref[frame] = both[:HALF]
        dk_ref[frame] = both[HALF:]
        values.append(
            jnp.concatenate(
                [
                    jnp.concatenate(
                        [item[HDIM:], swap(item[HDIM + 2 * FOLD - HDIM :])], axis=0
                    )
                    for item in items
                ],
                axis=0,
            )
        )
    both = jnp.where(low, values[0], swap(values[1])).T.astype(BF16)
    dv_ref[0] = both[:HALF]
    dv_ref[1] = both[HALF:]


def unpack(received):
    shape = jax.ShapeDtypeStruct((2, HALF, HEADS * HDIM), BF16)
    return pl.pallas_call(
        unpack_kernel,
        out_shape=(shape, shape, shape),
        in_specs=vmem_specs(1),
        out_specs=tuple(vmem_specs(3)),
        compiler_params=pltpu.CompilerParams(vmem_limit_bytes=LIMIT),
        name="spatial_unpack",
    )(received)


def frames_back(queries, keys_in, values, out_grad):
    scale = 1.0 / math.sqrt(queries.shape[-1])
    scores = (
        jnp.einsum("fthd,gthd->thfg", queries, keys_in, preferred_element_type=jnp.float32) * scale
    )
    peak = jnp.max(scores, axis=-1, keepdims=True)
    raised = jnp.exp(scores - peak)
    weights = raised / jnp.sum(raised, axis=-1, keepdims=True)
    prob_grad = jnp.einsum("fthd,gthd->thfg", out_grad, values, preferred_element_type=jnp.float32)
    inner = jnp.sum(weights * prob_grad, axis=-1, keepdims=True)
    score_low = (weights * (prob_grad - inner)).astype(jnp.bfloat16)
    weight_low = weights.astype(jnp.bfloat16)
    query_grad = (
        jnp.einsum("thfg,gthd->fthd", score_low, keys_in, preferred_element_type=jnp.float32)
        * scale
    )
    key_grad = (
        jnp.einsum("thfg,fthd->gthd", score_low, queries, preferred_element_type=jnp.float32)
        * scale
    )
    value_grad = jnp.einsum(
        "thfg,fthd->gthd", weight_low, out_grad, preferred_element_type=jnp.float32
    )
    output = jnp.einsum("thfg,gthd->fthd", weight_low, values, preferred_element_type=jnp.float32)
    return (
        query_grad.astype(jnp.bfloat16),
        key_grad.astype(jnp.bfloat16),
        value_grad.astype(jnp.bfloat16),
        output.astype(jnp.bfloat16),
    )


def space_perm(move):
    pairs = []
    for index in range(32):
        z, y, c = index // 8, (index // 2) % 4, index % 2
        z, y, c = move(z, y, c)
        pairs.append((index, (z % 4) * 8 + (y % 4) * 2 + c % 2))
    return pairs


def collect(block, own, moves, axis):
    size = len(moves) + 1
    out = jnp.zeros((size,) + block.shape, block.dtype)
    out = lax.dynamic_update_index_in_dim(out, block, own, 0)
    for shift, move in enumerate(moves, 1):
        got = lax.ppermute(block, axis, move)
        out = lax.dynamic_update_index_in_dim(out, got, lax.rem(own + size - shift, size), 0)
    return out


def sum_weight_grad(partial):
    rows, width = partial.shape
    blocks = partial.astype(BF16).reshape(4, 32, rows // 128, width).transpose(1, 0, 2, 3)
    got = lax.all_to_all(blocks, "space", split_axis=0, concat_axis=0, tiled=True)
    mine = jnp.sum(got.astype(F32), axis=0)
    dp = lax.axis_index("dp")
    total = lax.dynamic_index_in_dim(mine, dp, 0, keepdims=False)
    for shift in range(1, 4):
        send = lax.dynamic_index_in_dim(mine, lax.rem(dp + shift, 4), 0, keepdims=False)
        total = total + lax.ppermute(send, "dp", [(i, (i + shift) % 4) for i in range(4)])
    space = lax.axis_index("space")
    z, y, c = space // 8, lax.rem(space // 2, 4), lax.rem(space, 2)
    out = collect(total, z, [space_perm(lambda a, b, e, s=s: (a + s, b, e)) for s in (1, 2, 3)], "space")
    out = collect(out, y, [space_perm(lambda a, b, e, s=s: (a, b + s, e)) for s in (1, 2, 3)], "space")
    out = collect(out, c, [space_perm(lambda a, b, e: (a, b, e + 1))], "space")
    return out.transpose(2, 1, 0, 3, 4).reshape(rows // 4, width)


def shards(
    q_spatial,
    k_spatial,
    v_spatial,
    grad_spatial,
    q_temporal,
    k_temporal,
    v_temporal,
    grad_out,
    w_tout,
):
    packed = pack(q_spatial[0], k_spatial[0], v_spatial[0], grad_spatial[0])
    received = lax.all_to_all(packed, "space", split_axis=0, concat_axis=0, tiled=True)
    results = attend(received)
    returned = lax.all_to_all(results, "space", split_axis=0, concat_axis=0, tiled=True)
    dq, dk, dv = unpack(returned)

    heads_in = (
        lax.all_to_all(q_temporal, "tm", split_axis=3, concat_axis=1, tiled=True),
        lax.all_to_all(k_temporal, "tm", split_axis=3, concat_axis=1, tiled=True),
        lax.all_to_all(v_temporal, "tm", split_axis=3, concat_axis=1, tiled=True),
    )
    grad_all = lax.all_gather(grad_out, "tm", axis=1, tiled=True)
    width = grad_out.shape[3]
    all_frames = grad_all.shape[1]
    tokens = grad_all.shape[2]
    grad_rows = grad_all.reshape(all_frames * tokens, width)
    local_width = w_tout.shape[1]
    local_heads = local_width // HDIM
    head_grad = jnp.dot(
        grad_rows,
        lax.all_gather(w_tout, "dp", axis=0, tiled=True),
        preferred_element_type=jnp.float32,
    )

    def head_split(field):
        return field.reshape(all_frames, tokens, local_heads, HDIM)

    def head_join(field):
        return field.reshape(1, all_frames, tokens, local_width)

    temporal = frames_back(
        head_split(heads_in[0]),
        head_split(heads_in[1]),
        head_split(heads_in[2]),
        head_split(head_grad.astype(jnp.bfloat16)),
    )
    back = (
        lax.all_to_all(head_join(temporal[0]), "tm", split_axis=1, concat_axis=3, tiled=True),
        lax.all_to_all(head_join(temporal[1]), "tm", split_axis=1, concat_axis=3, tiled=True),
        lax.all_to_all(head_join(temporal[2]), "tm", split_axis=1, concat_axis=3, tiled=True),
    )
    output_rows = temporal[3].reshape(all_frames * tokens, local_width)
    weight_scale = 1.0 / math.sqrt(65536)
    partial = (
        lax.dot_general(
            grad_rows, output_rows, (((0,), (0,)), ((), ())), preferred_element_type=jnp.float32
        )
        * weight_scale
    )
    weight_grad = sum_weight_grad(partial)
    return (dq[None], dk[None], dv[None], back[0], back[1], back[2], weight_grad)


def solution(mesh):
    return jax.shard_map(
        shards,
        mesh=mesh,
        in_specs=(
            P("dp", "tm", "space", None),
            P("dp", "tm", "space", None),
            P("dp", "tm", "space", None),
            P("dp", "tm", "space", None),
            P("dp", "tm", "space", None),
            P("dp", "tm", "space", None),
            P("dp", "tm", "space", None),
            P("dp", "tm", "space", None),
            P("dp", "tm"),
        ),
        out_specs=(
            P("dp", "tm", "space", None),
            P("dp", "tm", "space", None),
            P("dp", "tm", "space", None),
            P("dp", "tm", "space", None),
            P("dp", "tm", "space", None),
            P("dp", "tm", "space", None),
            P("dp", "tm"),
        ),
        check_vma=False,
    )
```

```python
import math
import functools
import jax
import jax.numpy as jnp
from jax import lax
from jax.experimental import pallas as pl
from jax.experimental.pallas import tpu as pltpu
from jax.sharding import PartitionSpec as P

HEADS = 16
HDIM = 72
LANES = 128
HALF = 64
FOLD = 40
F32 = jnp.float32
BF16 = jnp.bfloat16
LIMIT = 56 * 1024 * 1024
LAST = (((1,), (1,)), ((), ()))


def vmem_specs(count):
    return [pl.BlockSpec(memory_space=pltpu.VMEM)] * count


def low_lanes(rows):
    return lax.broadcasted_iota(jnp.int32, (rows, LANES), 1) < HALF


def swap(block):
    return pltpu.roll(block, HALF, 1)


def pack_kernel(q_ref, k_ref, v_ref, g_ref, out_ref):
    for frame in range(2):
        for pair, (first, second) in enumerate(((q_ref, k_ref), (v_ref, g_ref))):
            rows = jnp.concatenate([first[frame], second[frame]], axis=0).astype(F32)
            columns = rows.T
            for head in range(HEADS):
                out_ref[frame * HEADS + head, pair] = columns[
                    head * HDIM : (head + 1) * HDIM
                ].astype(BF16)


def pack(q, k, v, g):
    return pl.pallas_call(
        pack_kernel,
        out_shape=jax.ShapeDtypeStruct((2 * HEADS, 2, HDIM, LANES), BF16),
        in_specs=vmem_specs(4),
        out_specs=pl.BlockSpec(memory_space=pltpu.VMEM),
        compiler_params=pltpu.CompilerParams(vmem_limit_bytes=LIMIT),
        name="spatial_pack",
    )(q, k, v, g)


def attend_kernel(
    in_ref, out_ref, q_t, k_t, g_t, q_n, k_n, v_n, g_n, s_buf, p_buf, dq_t, dk_n, dv_n, *, step
):
    length = q_t.shape[1]
    pairs = length // LANES
    scale = 1.0 / math.sqrt(HDIM)
    power = scale * math.log2(math.e)

    def split(j, pair):
        first = in_ref[2 * j, pair].astype(F32)
        second = in_ref[2 * j + 1, pair].astype(F32)
        low = low_lanes(HDIM)
        return (
            jnp.where(low, first, swap(second)),
            jnp.where(low, swap(first), second),
        )

    for j in range(pairs):
        at = slice(j * LANES, (j + 1) * LANES)
        q, k = split(j, 0)
        v, g = split(j, 1)
        q_t[:, at] = q.astype(BF16)
        k_t[:, at] = k.astype(BF16)
        g_t[:, at] = g.astype(BF16)
        q_n[at, :] = q.T.astype(BF16)
        k_n[at, :] = k.T.astype(BF16)
        v_n[at, :] = v.T.astype(BF16)
        g_n[at, :] = g.T.astype(BF16)

    blocks = length // step

    def products(i, slot):
        at = pl.ds(pl.multiple_of(i * step, step), step)
        s_buf[slot] = jnp.dot(k_n[...], q_t[:, at], preferred_element_type=F32)
        p_buf[slot] = jnp.dot(v_n[...], g_t[:, at], preferred_element_type=F32)

    def rest(i, slot, first):
        at = pl.ds(pl.multiple_of(i * step, step), step)
        scores = s_buf[slot]
        peak = jnp.max(scores, axis=0, keepdims=True)
        raised = jnp.exp2((scores - peak) * power)
        over = 1.0 / jnp.sum(raised, axis=0, keepdims=True)
        grads = p_buf[slot]
        inner = jnp.sum(raised * grads, axis=0, keepdims=True) * over
        weights = raised * over
        low_w = weights.astype(BF16)
        low_s = (weights * (grads - inner)).astype(BF16)
        dv = jnp.dot(low_w, g_n[at, :], preferred_element_type=F32)
        dk = jnp.dot(low_s, q_n[at, :], preferred_element_type=F32)
        if first:
            dv_n[...] = dv
            dk_n[...] = dk
        else:
            dv_n[...] += dv
            dk_n[...] += dk
        dq_t[:, at] = jnp.dot(k_t[...], low_s, preferred_element_type=F32) * scale

    products(0, 0)
    products(1, 1)
    rest(0, 0, True)

    def body(i, _):
        slot = lax.rem(i, 2)
        products(i + 1, 1 - slot)
        rest(i, slot, False)
        return 0

    lax.fori_loop(1, blocks - 1, body, 0)
    rest(blocks - 1, (blocks - 1) % 2, False)

    for j in range(pairs):
        at = slice(j * LANES, (j + 1) * LANES)
        dq = dq_t[:, at]
        dk = (dk_n[at, :] * scale).T
        dv = dv_n[at, :].T
        low = low_lanes(HDIM)
        low_f = low_lanes(FOLD)
        upper, lower = dv[:FOLD], dv[HDIM - FOLD :]
        out_ref[2 * j] = jnp.concatenate(
            [jnp.where(low, dq, swap(dk)), jnp.where(low_f, upper, swap(lower))], axis=0
        ).astype(BF16)
        out_ref[2 * j + 1] = jnp.concatenate(
            [jnp.where(low, swap(dq), dk), jnp.where(low_f, swap(upper), lower)], axis=0
        ).astype(BF16)


def attend(received, step=256):
    sources = received.shape[0]
    length = sources * HALF
    wide = pltpu.VMEM((HDIM, length), BF16)
    tall = pltpu.VMEM((length, HDIM), BF16)
    return pl.pallas_call(
        functools.partial(attend_kernel, step=step),
        out_shape=jax.ShapeDtypeStruct((sources, HDIM + FOLD, LANES), BF16),
        in_specs=vmem_specs(1),
        out_specs=pl.BlockSpec(memory_space=pltpu.VMEM),
        scratch_shapes=[
            wide, wide, wide, tall, tall, tall, tall,
            pltpu.VMEM((2, length, step), F32),
            pltpu.VMEM((2, length, step), F32),
            pltpu.VMEM((HDIM, length), F32),
            pltpu.VMEM((length, HDIM), F32),
            pltpu.VMEM((length, HDIM), F32),
        ],
        compiler_params=pltpu.CompilerParams(vmem_limit_bytes=LIMIT),
        cost_estimate=pl.CostEstimate(
            flops=10 * length * length * 256, bytes_accessed=2200000, transcendentals=length * length
        ),
        name="spatial_attention",
    )(received)


def unpack_kernel(in_ref, dq_ref, dk_ref, dv_ref):
    low = low_lanes(HEADS * HDIM)
    values = []
    for frame in range(2):
        items = [in_ref[frame * HEADS + head].astype(F32) for head in range(HEADS)]
        both = jnp.concatenate([item[:HDIM] for item in items], axis=0).T.astype(BF16)
        dq_ref[frame] = both[:HALF]
        dk_ref[frame] = both[HALF:]
        values.append(
            jnp.concatenate(
                [
                    jnp.concatenate(
                        [item[HDIM:], swap(item[HDIM + 2 * FOLD - HDIM :])], axis=0
                    )
                    for item in items
                ],
                axis=0,
            )
        )
    both = jnp.where(low, values[0], swap(values[1])).T.astype(BF16)
    dv_ref[0] = both[:HALF]
    dv_ref[1] = both[HALF:]


def unpack(received):
    shape = jax.ShapeDtypeStruct((2, HALF, HEADS * HDIM), BF16)
    return pl.pallas_call(
        unpack_kernel,
        out_shape=(shape, shape, shape),
        in_specs=vmem_specs(1),
        out_specs=tuple(vmem_specs(3)),
        compiler_params=pltpu.CompilerParams(vmem_limit_bytes=LIMIT),
        name="spatial_unpack",
    )(received)


def flip(block):
    return pltpu.roll(block, HALF, 1)


def send_pack_kernel(me_ref, q_ref, k_ref, v_ref, out0, out1, out2, out3, held):
    for part, ref in enumerate((q_ref, k_ref, v_ref)):
        rows = jnp.concatenate([ref[0], ref[1]], axis=0).astype(F32)
        columns = rows.T.astype(BF16)
        at = slice(part * LANES, (part + 1) * LANES)
        held[0, :, at] = columns[:288]
        held[1, :, at] = columns[288:576]
        held[2, :, at] = columns[576:864]
        held[3, :, at] = columns[864:]
    me = me_ref[0]
    for shift, out in enumerate((out0, out1, out2, out3)):
        out[...] = held[lax.rem(me + shift, 4)]


def send_pack(me, q, k, v):
    shape = jax.ShapeDtypeStruct((288, 3 * LANES), BF16)
    return pl.pallas_call(
        send_pack_kernel,
        out_shape=(shape,) * 4,
        in_specs=[pl.BlockSpec(memory_space=pltpu.SMEM)] + vmem_specs(3),
        out_specs=tuple(vmem_specs(4)),
        scratch_shapes=[pltpu.VMEM((4, 288, 3 * LANES), BF16)],
        compiler_params=pltpu.CompilerParams(vmem_limit_bytes=LIMIT),
        name="temporal_pack",
    )(me, q, k, v)


def rows_of(values):
    return jnp.concatenate([jnp.sum(value, axis=0, keepdims=True) for value in values], axis=0)


def frame_weights(query, keys):
    scores = rows_of([query * key for key in keys])
    peak = jnp.max(scores, axis=0, keepdims=True)
    raised = jnp.exp2((scores - peak) * (math.log2(math.e) / math.sqrt(HDIM)))
    return raised / jnp.sum(raised, axis=0, keepdims=True)


def rounded(value):
    return value.astype(BF16).astype(F32)


def head_rows(wide, head, part):
    rows = pl.ds(pl.multiple_of(head * HDIM, 8), HDIM)
    at = slice(part * LANES, (part + 1) * LANES)
    return [wide[shift, rows, at] for shift in range(4)]


def both_ways(blocks):
    out = []
    for block in blocks:
        out += [block, flip(block)]
    return out


def tout_kernel(me_ref, in0, in1, in2, in3, out_ref, wide, total):
    for shift, ref in enumerate((in0, in1, in2, in3)):
        wide[shift] = ref[...].astype(F32)

    def body(head, _):
        queries = head_rows(wide, head, 0)
        keys = both_ways(head_rows(wide, head, 1))
        values = both_ways(head_rows(wide, head, 2))
        for shift in range(4):
            weights = rounded(frame_weights(queries[shift], keys))
            out = weights[0:1] * values[0]
            for j in range(1, 8):
                out = out + weights[j : j + 1] * values[j]
            total[shift, pl.ds(pl.multiple_of(head * HDIM, 8), HDIM)] = out
        return 0

    lax.fori_loop(0, 4, body, 0)
    me = me_ref[0]
    for shift in range(4):
        out_ref[lax.rem(me + 4 - shift, 4)] = total[shift].astype(BF16)


def temporal_out(me, pieces):
    return pl.pallas_call(
        tout_kernel,
        out_shape=jax.ShapeDtypeStruct((4, 288, LANES), BF16),
        in_specs=[pl.BlockSpec(memory_space=pltpu.SMEM)] + vmem_specs(4),
        out_specs=pl.BlockSpec(memory_space=pltpu.VMEM),
        scratch_shapes=[
            pltpu.VMEM((4, 288, 3 * LANES), F32),
            pltpu.VMEM((4, 288, LANES), F32),
        ],
        compiler_params=pltpu.CompilerParams(vmem_limit_bytes=LIMIT),
        name="temporal_tout",
    )(me, *pieces)


def partial_kernel(tout_ref, grad_ref, out_ref, full, piece, *, scale):
    total = jnp.dot(tout_ref[0], grad_ref[0], preferred_element_type=F32)
    for a in range(1, 4):
        total = total + jnp.dot(tout_ref[a], grad_ref[a], preferred_element_type=F32)
    full[...] = total * scale
    piece[...] = jnp.zeros_like(piece)

    for s in range(32):
        for tile in range(9):
            at = slice(tile * LANES, (tile + 1) * LANES)
            piece[tile * 8 : tile * 8 + 8] = full[8 * s : 8 * s + 8, at]
            piece[72 + tile : 73 + tile] = full[256 + s : 257 + s, at]
        out_ref[s] = piece[...].astype(BF16)


def weight_partial(tout, grads, scale):
    return pl.pallas_call(
        functools.partial(partial_kernel, scale=scale),
        out_shape=jax.ShapeDtypeStruct((32, 96, LANES), BF16),
        in_specs=vmem_specs(2),
        out_specs=pl.BlockSpec(memory_space=pltpu.VMEM),
        scratch_shapes=[pltpu.VMEM((288, 1152), F32), pltpu.VMEM((96, LANES), F32)],
        compiler_params=pltpu.CompilerParams(vmem_limit_bytes=LIMIT),
        name="weight_partial",
    )(tout, grads)


def weight_sum_kernel(dp_ref, in_ref, keep_ref, send_ref, rows, parts):
    total = in_ref[0].astype(F32)
    for s in range(1, 32):
        total = total + in_ref[s].astype(F32)
    rows[8:16] = jnp.zeros((8, 1152), F32)
    for tile in range(9):
        at = slice(tile * LANES, (tile + 1) * LANES)
        rows[0:8, at] = total[tile * 8 : tile * 8 + 8]
        rows[8:9, at] = total[72 + tile : 73 + tile]
    for d in range(4):
        parts[d] = rows[:, d * 288 : (d + 1) * 288]
    dp = dp_ref[0]
    keep_ref[0] = parts[dp]
    keep_ref[1] = parts[lax.rem(dp + 2, 4)]
    other = dp + 1 - 2 * lax.rem(dp, 2)
    send_ref[0] = parts[other]
    send_ref[1] = parts[lax.rem(other + 2, 4)]


def weight_sum(dp, received):
    shape = jax.ShapeDtypeStruct((2, 16, 288), F32)
    return pl.pallas_call(
        weight_sum_kernel,
        out_shape=(shape, shape),
        in_specs=[pl.BlockSpec(memory_space=pltpu.SMEM)] + vmem_specs(1),
        out_specs=tuple(vmem_specs(2)),
        scratch_shapes=[pltpu.VMEM((16, 1152), F32), pltpu.VMEM((4, 16, 288), F32)],
        compiler_params=pltpu.CompilerParams(vmem_limit_bytes=LIMIT),
        name="weight_sum",
    )(dp, received)


def weight_share_kernel(mine_ref, got_ref, out_ref, wide, folded):
    wide[...] = jnp.zeros_like(wide)
    folded[...] = jnp.zeros_like(folded)
    wide[:, :288] = mine_ref[...] + got_ref[...]
    for tile in range(3):
        at = slice(tile * LANES, (tile + 1) * LANES)
        folded[tile * 8 : tile * 8 + 8] = wide[0:8, at]
        folded[24 + tile : 25 + tile] = wide[8:9, at]
    copy = folded[...].astype(BF16)
    for s in range(32):
        out_ref[s] = copy


def weight_share(mine, got):
    return pl.pallas_call(
        weight_share_kernel,
        out_shape=jax.ShapeDtypeStruct((32, 32, LANES), BF16),
        in_specs=vmem_specs(2),
        out_specs=pl.BlockSpec(memory_space=pltpu.VMEM),
        scratch_shapes=[pltpu.VMEM((16, 3 * LANES), F32), pltpu.VMEM((32, LANES), F32)],
        compiler_params=pltpu.CompilerParams(vmem_limit_bytes=LIMIT),
        name="weight_share",
    )(mine, got)


def weight_final_kernel(in_ref, out_ref, full):
    for s in range(32):
        block = in_ref[s].astype(F32)
        for tile in range(3):
            at = slice(tile * LANES, (tile + 1) * LANES)
            full[8 * s : 8 * s + 8, at] = block[tile * 8 : tile * 8 + 8]
            full[256 + s : 257 + s, at] = block[24 + tile : 25 + tile]
    out_ref[...] = full[...].T[:288]


def weight_final(gathered):
    return pl.pallas_call(
        weight_final_kernel,
        out_shape=jax.ShapeDtypeStruct((288, 288), F32),
        in_specs=vmem_specs(1),
        out_specs=pl.BlockSpec(memory_space=pltpu.VMEM),
        scratch_shapes=[pltpu.VMEM((288, 3 * LANES), F32)],
        compiler_params=pltpu.CompilerParams(vmem_limit_bytes=LIMIT),
        name="weight_final",
    )(gathered)


def temporal_kernel(
    me_ref, in0, in1, in2, in3, grad_ref, w_ref, out0, out1, out2, out3, wide, back
):
    me = me_ref[0]
    for shift, ref in enumerate((in0, in1, in2, in3)):
        wide[shift, :, : 3 * LANES] = ref[...].astype(F32)
        grads = grad_ref[lax.rem(me + 4 - shift, 4)]
        tgrad = rounded(jnp.dot(grads, w_ref[...], preferred_element_type=F32))
        wide[shift, :, 3 * LANES :] = tgrad.T
    scale = 1.0 / math.sqrt(HDIM)

    def body(head, _):
        rows = pl.ds(pl.multiple_of(head * HDIM, 8), HDIM)
        queries = head_rows(wide, head, 0)
        keys = both_ways(head_rows(wide, head, 1))
        values = both_ways(head_rows(wide, head, 2))
        grads = head_rows(wide, head, 3)
        low_w, low_s = [], []
        for shift in range(4):
            weights = frame_weights(queries[shift], keys)
            pgrad = rows_of([grads[shift] * value for value in values])
            inner = jnp.sum(weights * pgrad, axis=0, keepdims=True)
            low_w.append(rounded(weights))
            low_s.append(rounded(weights * (pgrad - inner)))
            dq = low_s[shift][0:1] * keys[0]
            for j in range(1, 8):
                dq = dq + low_s[shift][j : j + 1] * keys[j]
            back[shift, rows, 0:LANES] = dq * scale
        for b in range(4):
            for part, (coefs, terms, factor) in enumerate(
                ((low_s, queries, scale), (low_w, grads, 1.0)), 1
            ):
                sums = []
                for way in range(2):
                    j = 2 * b + way
                    total = coefs[0][j : j + 1] * terms[0]
                    for shift in range(1, 4):
                        total = total + coefs[shift][j : j + 1] * terms[shift]
                    sums.append(total)
                back[b, rows, part * LANES : (part + 1) * LANES] = (
                    sums[0] + flip(sums[1])
                ) * factor
        return 0

    lax.fori_loop(0, 4, body, 0)
    for shift, out in enumerate((out0, out1, out2, out3)):
        out[...] = back[shift].astype(BF16)


def temporal_back(me, pieces, grads, w):
    shape = jax.ShapeDtypeStruct((288, 3 * LANES), BF16)
    return pl.pallas_call(
        temporal_kernel,
        out_shape=(shape,) * 4,
        in_specs=[pl.BlockSpec(memory_space=pltpu.SMEM)] + vmem_specs(6),
        out_specs=tuple(vmem_specs(4)),
        scratch_shapes=[
            pltpu.VMEM((4, 288, 4 * LANES), F32),
            pltpu.VMEM((4, 288, 3 * LANES), F32),
        ],
        compiler_params=pltpu.CompilerParams(vmem_limit_bytes=LIMIT),
        name="temporal_back",
    )(me, *pieces, grads, w)


def receive_kernel(me_ref, in0, in1, in2, in3, dq_ref, dk_ref, dv_ref, held):
    me = me_ref[0]
    for shift, ref in enumerate((in0, in1, in2, in3)):
        held[lax.rem(me + shift, 4)] = ref[...]
    for part, out in enumerate((dq_ref, dk_ref, dv_ref)):
        at = slice(part * LANES, (part + 1) * LANES)
        columns = jnp.concatenate([held[t, :, at] for t in range(4)], axis=0).astype(F32)
        rows = columns.T.astype(BF16)
        out[0] = rows[:HALF]
        out[1] = rows[HALF:]


def receive(me, pieces):
    shape = jax.ShapeDtypeStruct((2, HALF, HEADS * HDIM), BF16)
    return pl.pallas_call(
        receive_kernel,
        out_shape=(shape,) * 3,
        in_specs=[pl.BlockSpec(memory_space=pltpu.SMEM)] + vmem_specs(4),
        out_specs=tuple(vmem_specs(3)),
        scratch_shapes=[pltpu.VMEM((4, 288, 3 * LANES), BF16)],
        compiler_params=pltpu.CompilerParams(vmem_limit_bytes=LIMIT),
        name="temporal_unpack",
    )(me, *pieces)


def space_perm(move):
    pairs = []
    for index in range(32):
        z, y, c = index // 8, (index // 2) % 4, index % 2
        z, y, c = move(z, y, c)
        pairs.append((index, (z % 4) * 8 + (y % 4) * 2 + c % 2))
    return pairs


Y_MOVES = [space_perm(lambda z, y, c, s=s: (z, y ^ s, c)) for s in (1, 2)]
C_MOVE = space_perm(lambda z, y, c: (z, y, c ^ 1))
SWAP = [[(i, i ^ s) for i in range(4)] for s in (1, 2)]
RING = [[(i, (i + s) % 4) for i in range(4)] for s in (1, 2, 3)]
RING_BACK = [[(i, (i - s) % 4) for i in range(4)] for s in (1, 2, 3)]


def pair_up(block, bit, move, axis):
    got = lax.ppermute(block, axis, move)
    low = jnp.where(bit == 0, block, got)
    high = jnp.where(bit == 0, got, block)
    return jnp.stack([low, high])


def gather_dp(w):
    space, dp = lax.axis_index("space"), lax.axis_index("dp")
    y, c = lax.rem(space // 2, 4), lax.rem(space, 2)
    own = lax.dynamic_index_in_dim(w.reshape(2, 4, 36, 288), c, 0, keepdims=False)
    own = lax.dynamic_index_in_dim(own, y, 0, keepdims=False)
    out = pair_up(own, lax.rem(dp, 2), SWAP[0], "dp")
    return pair_up(out, dp // 2, SWAP[1], "dp")


def gather_near(block):
    space = lax.axis_index("space")
    y, c = lax.rem(space // 2, 4), lax.rem(space, 2)
    out = pair_up(block, lax.rem(y, 2), Y_MOVES[0], "space")
    out = pair_up(out, y // 2, Y_MOVES[1], "space")
    out = pair_up(out, c, C_MOVE, "space")
    return out.transpose(3, 4, 0, 1, 2, 5, 6).reshape(1152, 288)


def shards(
    q_spatial,
    k_spatial,
    v_spatial,
    grad_spatial,
    q_temporal,
    k_temporal,
    v_temporal,
    grad_out,
    w_tout,
):
    me = lax.axis_index("tm").reshape(1)
    dp = lax.axis_index("dp").reshape(1)
    grads = lax.all_gather(grad_out, "tm", axis=1, tiled=True).reshape(4, LANES, 1152)
    packed = pack(q_spatial[0], k_spatial[0], v_spatial[0], grad_spatial[0])
    received = lax.all_to_all(packed, "space", split_axis=0, concat_axis=0, tiled=True)

    sends = send_pack(me, q_temporal[0], k_temporal[0], v_temporal[0])
    pieces = (sends[0],) + tuple(
        lax.ppermute(sends[shift], "tm", RING[shift - 1]) for shift in (1, 2, 3)
    )
    tout = temporal_out(me, pieces)
    partial = weight_partial(tout, grads, 1.0 / math.sqrt(65536))
    weight = gather_dp(w_tout)

    received, partial = lax.optimization_barrier((received, partial))
    summed = lax.all_to_all(partial, "space", split_axis=0, concat_axis=0, tiled=True)
    results = attend(received)
    results, summed, weight, *pieces = lax.optimization_barrier((results, summed, weight) + pieces)
    returned = lax.all_to_all(results, "space", split_axis=0, concat_axis=0, tiled=True)

    keep, send = weight_sum(dp, summed)
    keep = keep + lax.ppermute(send, "dp", SWAP[0])
    shared = weight_share(keep[0], lax.ppermute(keep[1], "dp", SWAP[1]))

    backs = temporal_back(me, pieces, grads, gather_near(weight))
    shared, returned = lax.optimization_barrier((shared, returned))
    gathered = lax.all_to_all(shared, "space", split_axis=0, concat_axis=0, tiled=True)
    homes = (backs[0],) + tuple(
        lax.ppermute(backs[shift], "tm", RING_BACK[shift - 1]) for shift in (1, 2, 3)
    )
    dq_t, dk_t, dv_t = receive(me, homes)
    dq, dk, dv = unpack(returned)
    weight_grad = weight_final(gathered)
    return (dq[None], dk[None], dv[None], dq_t[None], dk_t[None], dv_t[None], weight_grad)


def solution(mesh):
    return jax.shard_map(
        shards,
        mesh=mesh,
        in_specs=(
            P("dp", "tm", "space", None),
            P("dp", "tm", "space", None),
            P("dp", "tm", "space", None),
            P("dp", "tm", "space", None),
            P("dp", "tm", "space", None),
            P("dp", "tm", "space", None),
            P("dp", "tm", "space", None),
            P("dp", "tm", "space", None),
            P("dp", "tm"),
        ),
        out_specs=(
            P("dp", "tm", "space", None),
            P("dp", "tm", "space", None),
            P("dp", "tm", "space", None),
            P("dp", "tm", "space", None),
            P("dp", "tm", "space", None),
            P("dp", "tm", "space", None),
            P("dp", "tm"),
        ),
        check_vma=False,
    )
```

```python
import math
import functools
import jax
import jax.numpy as jnp
from jax import lax
from jax.experimental import pallas as pl
from jax.experimental.pallas import tpu as pltpu
from jax.sharding import PartitionSpec as P

HEADS = 16
HDIM = 72
LANES = 128
HALF = 64
FOLD = 40
F32 = jnp.float32
BF16 = jnp.bfloat16
LIMIT = 56 * 1024 * 1024
LAST = (((1,), (1,)), ((), ()))


def vmem_specs(count):
    return [pl.BlockSpec(memory_space=pltpu.VMEM)] * count


def low_lanes(rows):
    return lax.broadcasted_iota(jnp.int32, (rows, LANES), 1) < HALF


def swap(block):
    return pltpu.roll(block, HALF, 1)


def pack_kernel(q_ref, k_ref, v_ref, g_ref, out_ref):
    for frame in range(2):
        for pair, (first, second) in enumerate(((q_ref, k_ref), (v_ref, g_ref))):
            rows = jnp.concatenate([first[frame], second[frame]], axis=0).astype(F32)
            columns = rows.T
            for head in range(HEADS):
                out_ref[frame * HEADS + head, pair] = columns[
                    head * HDIM : (head + 1) * HDIM
                ].astype(BF16)


def pack(q, k, v, g):
    return pl.pallas_call(
        pack_kernel,
        out_shape=jax.ShapeDtypeStruct((2 * HEADS, 2, HDIM, LANES), BF16),
        in_specs=vmem_specs(4),
        out_specs=pl.BlockSpec(memory_space=pltpu.VMEM),
        compiler_params=pltpu.CompilerParams(vmem_limit_bytes=LIMIT),
        name="spatial_pack",
    )(q, k, v, g)


def attend_kernel(
    in_ref, out_ref, q_t, k_t, g_t, q_n, k_n, v_n, g_n, s_buf, p_buf, dq_t, dk_n, dv_n, *, step
):
    length = q_t.shape[1]
    pairs = length // LANES
    scale = 1.0 / math.sqrt(HDIM)
    power = scale * math.log2(math.e)

    def split(j, pair):
        first = in_ref[2 * j, pair].astype(F32)
        second = in_ref[2 * j + 1, pair].astype(F32)
        low = low_lanes(HDIM)
        return (
            jnp.where(low, first, swap(second)),
            jnp.where(low, swap(first), second),
        )

    for j in range(pairs):
        at = slice(j * LANES, (j + 1) * LANES)
        q, k = split(j, 0)
        v, g = split(j, 1)
        q_t[:, at] = q.astype(BF16)
        k_t[:, at] = k.astype(BF16)
        g_t[:, at] = g.astype(BF16)
        q_n[at, :] = q.T.astype(BF16)
        k_n[at, :] = k.T.astype(BF16)
        v_n[at, :] = v.T.astype(BF16)
        g_n[at, :] = g.T.astype(BF16)

    blocks = length // step

    def products(i, slot):
        at = pl.ds(pl.multiple_of(i * step, step), step)
        s_buf[slot] = jnp.dot(k_n[...], q_t[:, at], preferred_element_type=F32)
        p_buf[slot] = jnp.dot(v_n[...], g_t[:, at], preferred_element_type=F32)

    def rest(i, slot, first):
        at = pl.ds(pl.multiple_of(i * step, step), step)
        scores = s_buf[slot]
        peak = jnp.max(scores, axis=0, keepdims=True)
        raised = jnp.exp2((scores - peak) * power)
        over = 1.0 / jnp.sum(raised, axis=0, keepdims=True)
        grads = p_buf[slot]
        inner = jnp.sum(raised * grads, axis=0, keepdims=True) * over
        weights = raised * over
        low_w = weights.astype(BF16)
        low_s = (weights * (grads - inner)).astype(BF16)
        dv = jnp.dot(low_w, g_n[at, :], preferred_element_type=F32)
        dk = jnp.dot(low_s, q_n[at, :], preferred_element_type=F32)
        if first:
            dv_n[...] = dv
            dk_n[...] = dk
        else:
            dv_n[...] += dv
            dk_n[...] += dk
        dq_t[:, at] = jnp.dot(k_t[...], low_s, preferred_element_type=F32) * scale

    products(0, 0)
    products(1, 1)
    rest(0, 0, True)

    def body(i, _):
        slot = lax.rem(i, 2)
        products(i + 1, 1 - slot)
        rest(i, slot, False)
        return 0

    lax.fori_loop(1, blocks - 1, body, 0)
    rest(blocks - 1, (blocks - 1) % 2, False)

    for j in range(pairs):
        at = slice(j * LANES, (j + 1) * LANES)
        dq = dq_t[:, at]
        dk = (dk_n[at, :] * scale).T
        dv = dv_n[at, :].T
        low = low_lanes(HDIM)
        low_f = low_lanes(FOLD)
        upper, lower = dv[:FOLD], dv[HDIM - FOLD :]
        out_ref[2 * j] = jnp.concatenate(
            [jnp.where(low, dq, swap(dk)), jnp.where(low_f, upper, swap(lower))], axis=0
        ).astype(BF16)
        out_ref[2 * j + 1] = jnp.concatenate(
            [jnp.where(low, swap(dq), dk), jnp.where(low_f, swap(upper), lower)], axis=0
        ).astype(BF16)


def attend(received, step=256):
    sources = received.shape[0]
    length = sources * HALF
    wide = pltpu.VMEM((HDIM, length), BF16)
    tall = pltpu.VMEM((length, HDIM), BF16)
    return pl.pallas_call(
        functools.partial(attend_kernel, step=step),
        out_shape=jax.ShapeDtypeStruct((sources, HDIM + FOLD, LANES), BF16),
        in_specs=vmem_specs(1),
        out_specs=pl.BlockSpec(memory_space=pltpu.VMEM),
        scratch_shapes=[
            wide, wide, wide, tall, tall, tall, tall,
            pltpu.VMEM((2, length, step), F32),
            pltpu.VMEM((2, length, step), F32),
            pltpu.VMEM((HDIM, length), F32),
            pltpu.VMEM((length, HDIM), F32),
            pltpu.VMEM((length, HDIM), F32),
        ],
        compiler_params=pltpu.CompilerParams(vmem_limit_bytes=LIMIT),
        cost_estimate=pl.CostEstimate(
            flops=10 * length * length * 256, bytes_accessed=2200000, transcendentals=length * length
        ),
        name="spatial_attention",
    )(received)


def unpack_kernel(in_ref, dq_ref, dk_ref, dv_ref, dw_ref, full):
    low = low_lanes(HEADS * HDIM)
    values = []
    for frame in range(2):
        items = [
            in_ref[frame * HEADS + head, : HDIM + FOLD].astype(F32) for head in range(HEADS)
        ]
        both = jnp.concatenate([item[:HDIM] for item in items], axis=0).T.astype(BF16)
        dq_ref[frame] = both[:HALF]
        dk_ref[frame] = both[HALF:]
        values.append(
            jnp.concatenate(
                [
                    jnp.concatenate([item[HDIM:], swap(item[2 * FOLD :])], axis=0)
                    for item in items
                ],
                axis=0,
            )
        )
    both = jnp.where(low, values[0], swap(values[1])).T.astype(BF16)
    dv_ref[0] = both[:HALF]
    dv_ref[1] = both[HALF:]
    for s in range(2 * HEADS):
        block = in_ref[s, HDIM + FOLD :].astype(F32)
        start = 144 * (s % 2) + 8 * (s // 2)
        for tile in range(3):
            at = slice(tile * LANES, (tile + 1) * LANES)
            full[start : start + 8, at] = block[tile * 8 : tile * 8 + 8]
        start = 144 * (s % 2) + 128 + s // 2
        for r in range(3):
            full[start : start + 1, 96 * r : 96 * r + 96] = block[16 + r : 17 + r, 32:]
    dw_ref[...] = full[...].T[:288]


def unpack(received):
    shape = jax.ShapeDtypeStruct((2, HALF, HEADS * HDIM), BF16)
    return pl.pallas_call(
        unpack_kernel,
        out_shape=(shape, shape, shape, jax.ShapeDtypeStruct((288, 288), F32)),
        in_specs=vmem_specs(1),
        out_specs=tuple(vmem_specs(4)),
        scratch_shapes=[pltpu.VMEM((288, 3 * LANES), F32)],
        compiler_params=pltpu.CompilerParams(vmem_limit_bytes=LIMIT),
        name="spatial_unpack",
    )(received)


def flip(block):
    return pltpu.roll(block, HALF, 1)


def send_pack_kernel(me_ref, q_ref, k_ref, v_ref, w_ref, out0, out1, out2, out3, slice_ref, held):
    slice_ref[...] = w_ref[me_ref[1]]
    for part, ref in enumerate((q_ref, k_ref, v_ref)):
        rows = jnp.concatenate([ref[0], ref[1]], axis=0).astype(F32)
        columns = rows.T.astype(BF16)
        at = slice(part * LANES, (part + 1) * LANES)
        held[0, :, at] = columns[:288]
        held[1, :, at] = columns[288:576]
        held[2, :, at] = columns[576:864]
        held[3, :, at] = columns[864:]
    me = me_ref[0]
    for shift, out in enumerate((out0, out1, out2, out3)):
        out[...] = held[lax.rem(me + shift, 4)]


def send_pack(me, q, k, v, w):
    shape = jax.ShapeDtypeStruct((288, 3 * LANES), BF16)
    part = jax.ShapeDtypeStruct((36, 288), BF16)
    return pl.pallas_call(
        send_pack_kernel,
        out_shape=(shape,) * 4 + (part,),
        in_specs=[pl.BlockSpec(memory_space=pltpu.SMEM)] + vmem_specs(4),
        out_specs=tuple(vmem_specs(5)),
        scratch_shapes=[pltpu.VMEM((4, 288, 3 * LANES), BF16)],
        compiler_params=pltpu.CompilerParams(vmem_limit_bytes=LIMIT),
        name="temporal_pack",
    )(me, q, k, v, w)


def rows_of(values):
    return jnp.concatenate([jnp.sum(value, axis=0, keepdims=True) for value in values], axis=0)


def frame_weights(query, keys):
    scores = rows_of([query * key for key in keys])
    peak = jnp.max(scores, axis=0, keepdims=True)
    raised = jnp.exp2((scores - peak) * (math.log2(math.e) / math.sqrt(HDIM)))
    return raised / jnp.sum(raised, axis=0, keepdims=True)


def rounded(value):
    return value.astype(BF16).astype(F32)


def head_rows(wide, head, part):
    rows = pl.ds(pl.multiple_of(head * HDIM, 8), HDIM)
    at = slice(part * LANES, (part + 1) * LANES)
    return [wide[shift, rows, at] for shift in range(4)]


def both_ways(blocks):
    out = []
    for block in blocks:
        out += [block, flip(block)]
    return out


def pair_up(bit, own_ref, got_ref, out_ref):
    out_ref[bit] = own_ref[...]
    out_ref[1 - bit] = got_ref[...]


def tout_kernel(me_ref, in0, in1, in2, in3, own_ref, got_ref, out_ref, w_ref, wide, total):
    pair_up(lax.rem(me_ref[2], 2), own_ref, got_ref, w_ref)
    for shift, ref in enumerate((in0, in1, in2, in3)):
        wide[shift] = ref[...].astype(F32)

    def body(head, _):
        queries = head_rows(wide, head, 0)
        keys = both_ways(head_rows(wide, head, 1))
        values = both_ways(head_rows(wide, head, 2))
        for shift in range(4):
            weights = rounded(frame_weights(queries[shift], keys))
            out = weights[0:1] * values[0]
            for j in range(1, 8):
                out = out + weights[j : j + 1] * values[j]
            total[shift, pl.ds(pl.multiple_of(head * HDIM, 8), HDIM)] = out
        return 0

    lax.fori_loop(0, 4, body, 0)
    me = me_ref[0]
    for shift in range(4):
        out_ref[lax.rem(me + 4 - shift, 4)] = total[shift].astype(BF16)


def temporal_out(me, pieces, own, got):
    return pl.pallas_call(
        tout_kernel,
        out_shape=(
            jax.ShapeDtypeStruct((4, 288, LANES), BF16),
            jax.ShapeDtypeStruct((2, 36, 288), BF16),
        ),
        in_specs=[pl.BlockSpec(memory_space=pltpu.SMEM)] + vmem_specs(6),
        out_specs=tuple(vmem_specs(2)),
        scratch_shapes=[
            pltpu.VMEM((4, 288, 3 * LANES), F32),
            pltpu.VMEM((4, 288, LANES), F32),
        ],
        compiler_params=pltpu.CompilerParams(vmem_limit_bytes=LIMIT),
        name="temporal_tout",
    )(me, *pieces, own, got)


def partial_kernel(
    me_ref, tout_ref, grad_ref, own_ref, got_ref, keep_ref, send_ref, w_ref, full, *, scale
):
    pair_up(me_ref[2] // 2, own_ref, got_ref, w_ref)
    total = jnp.dot(tout_ref[0], grad_ref[0], preferred_element_type=F32)
    for a in range(1, 4):
        total = total + jnp.dot(tout_ref[a], grad_ref[a], preferred_element_type=F32)
    total = total * scale
    full[0] = total[:144]
    full[1] = total[144:]
    core = me_ref[3]
    keep_ref[...] = full[core]
    send_ref[...] = full[1 - core].astype(BF16)


def weight_partial(me, tout, grads, own, got, scale):
    return pl.pallas_call(
        functools.partial(partial_kernel, scale=scale),
        out_shape=(
            jax.ShapeDtypeStruct((144, 1152), F32),
            jax.ShapeDtypeStruct((144, 1152), BF16),
            jax.ShapeDtypeStruct((2, 2, 36, 288), BF16),
        ),
        in_specs=[pl.BlockSpec(memory_space=pltpu.SMEM)] + vmem_specs(4),
        out_specs=tuple(vmem_specs(3)),
        scratch_shapes=[pltpu.VMEM((2, 144, 1152), F32)],
        compiler_params=pltpu.CompilerParams(vmem_limit_bytes=LIMIT),
        name="weight_partial",
    )(me, tout, grads, own, got)


def weight_split_kernel(keep_ref, got_ref, out_ref, full, part):
    full[...] = keep_ref[...] + got_ref[...].astype(F32)
    part[...] = jnp.zeros_like(part)
    row = lax.broadcasted_iota(jnp.int32, (16, 8, LANES), 1)
    for d in range(4):
        part[:, :288] = full[:, d * 288 : (d + 1) * 288]
        tiles = [
            part[:128, tile * LANES : (tile + 1) * LANES].reshape(16, 8, LANES)
            for tile in range(3)
        ]
        rest = part[128:144, :]
        for r in range(3):
            moved = jnp.concatenate(
                [jnp.zeros((16, 32), F32), rest[:, 96 * r : 96 * r + 96]], axis=1
            )
            tiles[2] = tiles[2] + jnp.where(row == r, moved[:, None, :], 0.0)
        out_ref[d * 16 : (d + 1) * 16] = jnp.concatenate(tiles, axis=1).astype(BF16)


def weight_split(keep, got):
    return pl.pallas_call(
        weight_split_kernel,
        out_shape=jax.ShapeDtypeStruct((64, 24, LANES), BF16),
        in_specs=vmem_specs(2),
        out_specs=pl.BlockSpec(memory_space=pltpu.VMEM),
        scratch_shapes=[pltpu.VMEM((144, 1152), F32), pltpu.VMEM((144, 3 * LANES), F32)],
        compiler_params=pltpu.CompilerParams(vmem_limit_bytes=LIMIT),
        name="weight_split",
    )(keep, got)


def weight_join_kernel(spatial_ref, in_ref, out_ref):
    total = in_ref[0].astype(F32)
    for s in range(1, 64):
        total = total + in_ref[s].astype(F32)
    copy = total.astype(BF16)
    for s in range(32):
        out_ref[s, : HDIM + FOLD] = spatial_ref[s]
        out_ref[s, HDIM + FOLD :] = copy


def weight_join(spatial, received):
    return pl.pallas_call(
        weight_join_kernel,
        out_shape=jax.ShapeDtypeStruct((32, HDIM + FOLD + 24, LANES), BF16),
        in_specs=vmem_specs(2),
        out_specs=pl.BlockSpec(memory_space=pltpu.VMEM),
        compiler_params=pltpu.CompilerParams(vmem_limit_bytes=LIMIT),
        name="weight_join",
    )(spatial, received)


def temporal_kernel(
    me_ref, in0, in1, in2, in3, grad_ref, w_ref, out0, out1, out2, out3, wide, back
):
    me = me_ref[0]
    for shift, ref in enumerate((in0, in1, in2, in3)):
        wide[shift, :, : 3 * LANES] = ref[...].astype(F32)
        grads = grad_ref[lax.rem(me + 4 - shift, 4)]
        tgrad = rounded(jnp.dot(grads, w_ref[...], preferred_element_type=F32))
        wide[shift, :, 3 * LANES :] = tgrad.T
    scale = 1.0 / math.sqrt(HDIM)

    def body(head, _):
        rows = pl.ds(pl.multiple_of(head * HDIM, 8), HDIM)
        queries = head_rows(wide, head, 0)
        keys = both_ways(head_rows(wide, head, 1))
        values = both_ways(head_rows(wide, head, 2))
        grads = head_rows(wide, head, 3)
        low_w, low_s = [], []
        for shift in range(4):
            weights = frame_weights(queries[shift], keys)
            pgrad = rows_of([grads[shift] * value for value in values])
            inner = jnp.sum(weights * pgrad, axis=0, keepdims=True)
            low_w.append(rounded(weights))
            low_s.append(rounded(weights * (pgrad - inner)))
            dq = low_s[shift][0:1] * keys[0]
            for j in range(1, 8):
                dq = dq + low_s[shift][j : j + 1] * keys[j]
            back[shift, rows, 0:LANES] = dq * scale
        for b in range(4):
            for part, (coefs, terms, factor) in enumerate(
                ((low_s, queries, scale), (low_w, grads, 1.0)), 1
            ):
                sums = []
                for way in range(2):
                    j = 2 * b + way
                    total = coefs[0][j : j + 1] * terms[0]
                    for shift in range(1, 4):
                        total = total + coefs[shift][j : j + 1] * terms[shift]
                    sums.append(total)
                back[b, rows, part * LANES : (part + 1) * LANES] = (
                    sums[0] + flip(sums[1])
                ) * factor
        return 0

    lax.fori_loop(0, 4, body, 0)
    for shift, out in enumerate((out0, out1, out2, out3)):
        out[...] = back[shift].astype(BF16)


def temporal_back(me, pieces, grads, w):
    shape = jax.ShapeDtypeStruct((288, 3 * LANES), BF16)
    return pl.pallas_call(
        temporal_kernel,
        out_shape=(shape,) * 4,
        in_specs=[pl.BlockSpec(memory_space=pltpu.SMEM)] + vmem_specs(6),
        out_specs=tuple(vmem_specs(4)),
        scratch_shapes=[
            pltpu.VMEM((4, 288, 4 * LANES), F32),
            pltpu.VMEM((4, 288, 3 * LANES), F32),
        ],
        compiler_params=pltpu.CompilerParams(vmem_limit_bytes=LIMIT),
        name="temporal_back",
    )(me, *pieces, grads, w)


def receive_kernel(me_ref, in0, in1, in2, in3, dq_ref, dk_ref, dv_ref, held):
    me = me_ref[0]
    for shift, ref in enumerate((in0, in1, in2, in3)):
        held[lax.rem(me + shift, 4)] = ref[...]
    for part, out in enumerate((dq_ref, dk_ref, dv_ref)):
        at = slice(part * LANES, (part + 1) * LANES)
        columns = jnp.concatenate([held[t, :, at] for t in range(4)], axis=0).astype(F32)
        rows = columns.T.astype(BF16)
        out[0] = rows[:HALF]
        out[1] = rows[HALF:]


def receive(me, pieces):
    shape = jax.ShapeDtypeStruct((2, HALF, HEADS * HDIM), BF16)
    return pl.pallas_call(
        receive_kernel,
        out_shape=(shape,) * 3,
        in_specs=[pl.BlockSpec(memory_space=pltpu.SMEM)] + vmem_specs(4),
        out_specs=tuple(vmem_specs(3)),
        scratch_shapes=[pltpu.VMEM((4, 288, 3 * LANES), BF16)],
        compiler_params=pltpu.CompilerParams(vmem_limit_bytes=LIMIT),
        name="temporal_unpack",
    )(me, *pieces)


SWAP = [[(i, i ^ s) for i in range(4)] for s in (1, 2)]
SWAP_CORE = [(0, 1), (1, 0)]
RING = [[(i, (i + s) % 4) for i in range(4)] for s in (1, 2, 3)]
RING_BACK = [[(i, (i - s) % 4) for i in range(4)] for s in (1, 2, 3)]


def gather_near(block):
    y, c = lax.axis_index("y"), lax.axis_index("c")
    for bit, move, axis in ((lax.rem(y, 2), SWAP[0], "y"), (y // 2, SWAP[1], "y"), (c, SWAP_CORE, "c")):
        got = lax.ppermute(block, axis, move)
        block = jnp.stack([jnp.where(bit == 0, block, got), jnp.where(bit == 0, got, block)])
    return block.transpose(3, 4, 0, 1, 2, 5, 6).reshape(1152, 288)


def shards(
    q_spatial,
    k_spatial,
    v_spatial,
    grad_spatial,
    q_temporal,
    k_temporal,
    v_temporal,
    grad_out,
    w_tout,
):
    y, c = lax.axis_index("y"), lax.axis_index("c")
    me = jnp.stack([lax.axis_index("tm"), 4 * c + y, lax.axis_index("dp"), c])
    space = ("z", "y", "c")
    grads = lax.all_gather(grad_out, "tm", axis=1, tiled=True).reshape(4, LANES, 1152)
    packed = pack(q_spatial[0], k_spatial[0], v_spatial[0], grad_spatial[0])
    packed, q, k, v, w = lax.optimization_barrier(
        (packed, q_temporal[0], k_temporal[0], v_temporal[0], w_tout.reshape(8, 36, 288))
    )
    received = lax.all_to_all(packed, space, split_axis=0, concat_axis=0, tiled=True)

    *sends, own = send_pack(me, q, k, v, w)
    got = lax.ppermute(own, "dp", SWAP[0])
    pieces = (sends[0],) + tuple(
        lax.ppermute(sends[shift], "tm", RING[shift - 1]) for shift in (1, 2, 3)
    )
    tout, own = temporal_out(me, pieces, own, got)
    got = lax.ppermute(own, "dp", SWAP[1])
    keep, send, weight = weight_partial(me, tout, grads, own, got, 1.0 / math.sqrt(65536))
    blocks = weight_split(keep, lax.ppermute(send, "c", SWAP_CORE))

    received, blocks = lax.optimization_barrier((received, blocks))
    blocks = lax.all_to_all(blocks, ("dp", "z", "y"), split_axis=0, concat_axis=0, tiled=True)
    results = attend(received)
    results, weight, *pieces = lax.optimization_barrier((results, weight) + pieces)
    results = weight_join(results, blocks)
    returned = lax.all_to_all(results, space, split_axis=0, concat_axis=0, tiled=True)

    backs = temporal_back(me, pieces, grads, gather_near(weight))
    homes = (backs[0],) + tuple(
        lax.ppermute(backs[shift], "tm", RING_BACK[shift - 1]) for shift in (1, 2, 3)
    )
    dq_t, dk_t, dv_t = receive(me, homes)
    dq, dk, dv, weight_grad = unpack(returned)
    return (dq[None], dk[None], dv[None], dq_t[None], dk_t[None], dv_t[None], weight_grad)


def solution(mesh):
    sizes = (mesh.shape["dp"], mesh.shape["tm"], 4, 4, 2)
    split = jax.sharding.Mesh(mesh.devices.reshape(sizes), ("dp", "tm", "z", "y", "c"))
    field = P("dp", "tm", ("z", "y", "c"), None)
    return jax.shard_map(
        shards,
        mesh=split,
        in_specs=(field,) * 8 + (P("dp", "tm"),),
        out_specs=(field,) * 6 + (P("dp", "tm"),),
        check_vma=False,
    )
```

```python
import math
import functools
import jax
import jax.numpy as jnp
from jax import lax
from jax.experimental import pallas as pl
from jax.experimental.pallas import tpu as pltpu
from jax.sharding import PartitionSpec as P

HEADS = 16
HDIM = 72
LANES = 128
HALF = 64
FOLD = 40
F32 = jnp.float32
BF16 = jnp.bfloat16
LIMIT = 56 * 1024 * 1024
LAST = (((1,), (1,)), ((), ()))


def vmem_specs(count):
    return [pl.BlockSpec(memory_space=pltpu.VMEM)] * count


def low_lanes(rows):
    return lax.broadcasted_iota(jnp.int32, (rows, LANES), 1) < HALF


def swap(block):
    return pltpu.roll(block, HALF, 1)


def pack_kernel(q_ref, k_ref, v_ref, g_ref, out_ref):
    for frame in range(2):
        for pair, (first, second) in enumerate(((q_ref, k_ref), (v_ref, g_ref))):
            rows = jnp.concatenate([first[frame], second[frame]], axis=0).astype(F32)
            columns = rows.T
            for head in range(HEADS):
                out_ref[frame * HEADS + head, pair] = columns[
                    head * HDIM : (head + 1) * HDIM
                ].astype(BF16)


def pack(q, k, v, g):
    return pl.pallas_call(
        pack_kernel,
        out_shape=jax.ShapeDtypeStruct((2 * HEADS, 2, HDIM, LANES), BF16),
        in_specs=vmem_specs(4),
        out_specs=pl.BlockSpec(memory_space=pltpu.VMEM),
        compiler_params=pltpu.CompilerParams(vmem_limit_bytes=LIMIT),
        name="spatial_pack",
    )(q, k, v, g)


def attend_kernel(
    in_ref, out_ref, q_t, k_t, g_t, q_n, k_n, v_n, g_n, s_buf, p_buf, dq_t, dk_n, dv_n, *, step
):
    length = q_t.shape[1]
    pairs = length // LANES
    scale = 1.0 / math.sqrt(HDIM)
    power = scale * math.log2(math.e)

    def split(j, pair):
        first = in_ref[2 * j, pair].astype(F32)
        second = in_ref[2 * j + 1, pair].astype(F32)
        low = low_lanes(HDIM)
        return (
            jnp.where(low, first, swap(second)),
            jnp.where(low, swap(first), second),
        )

    for j in range(pairs):
        at = slice(j * LANES, (j + 1) * LANES)
        q, k = split(j, 0)
        v, g = split(j, 1)
        q_t[:, at] = q.astype(BF16)
        k_t[:, at] = k.astype(BF16)
        g_t[:, at] = g.astype(BF16)
        q_n[at, :] = q.T.astype(BF16)
        k_n[at, :] = k.T.astype(BF16)
        v_n[at, :] = v.T.astype(BF16)
        g_n[at, :] = g.T.astype(BF16)

    blocks = length // step

    def products(i, slot):
        at = pl.ds(pl.multiple_of(i * step, step), step)
        s_buf[slot] = jnp.dot(k_n[...], q_t[:, at], preferred_element_type=F32)
        p_buf[slot] = jnp.dot(v_n[...], g_t[:, at], preferred_element_type=F32)

    def rest(i, slot, first):
        at = pl.ds(pl.multiple_of(i * step, step), step)
        scores = s_buf[slot]
        peak = jnp.max(scores, axis=0, keepdims=True)
        raised = jnp.exp2((scores - peak) * power)
        over = 1.0 / jnp.sum(raised, axis=0, keepdims=True)
        grads = p_buf[slot]
        inner = jnp.sum(raised * grads, axis=0, keepdims=True) * over
        weights = raised * over
        low_w = weights.astype(BF16)
        low_s = (weights * (grads - inner)).astype(BF16)
        dv = jnp.dot(low_w, g_n[at, :], preferred_element_type=F32)
        dk = jnp.dot(low_s, q_n[at, :], preferred_element_type=F32)
        if first:
            dv_n[...] = dv
            dk_n[...] = dk
        else:
            dv_n[...] += dv
            dk_n[...] += dk
        dq_t[:, at] = jnp.dot(k_t[...], low_s, preferred_element_type=F32) * scale

    products(0, 0)
    products(1, 1)
    rest(0, 0, True)

    def body(i, _):
        slot = lax.rem(i, 2)
        products(i + 1, 1 - slot)
        rest(i, slot, False)
        return 0

    lax.fori_loop(1, blocks - 1, body, 0)
    rest(blocks - 1, (blocks - 1) % 2, False)

    for j in range(pairs):
        at = slice(j * LANES, (j + 1) * LANES)
        dq = dq_t[:, at]
        dk = (dk_n[at, :] * scale).T
        dv = dv_n[at, :].T
        low = low_lanes(HDIM)
        low_f = low_lanes(FOLD)
        upper, lower = dv[:FOLD], dv[HDIM - FOLD :]
        out_ref[2 * j] = jnp.concatenate(
            [jnp.where(low, dq, swap(dk)), jnp.where(low_f, upper, swap(lower))], axis=0
        ).astype(BF16)
        out_ref[2 * j + 1] = jnp.concatenate(
            [jnp.where(low, swap(dq), dk), jnp.where(low_f, swap(upper), lower)], axis=0
        ).astype(BF16)


def attend(received, step=256):
    sources = received.shape[0]
    length = sources * HALF
    wide = pltpu.VMEM((HDIM, length), BF16)
    tall = pltpu.VMEM((length, HDIM), BF16)
    return pl.pallas_call(
        functools.partial(attend_kernel, step=step),
        out_shape=jax.ShapeDtypeStruct((sources, HDIM + FOLD, LANES), BF16),
        in_specs=vmem_specs(1),
        out_specs=pl.BlockSpec(memory_space=pltpu.VMEM),
        scratch_shapes=[
            wide, wide, wide, tall, tall, tall, tall,
            pltpu.VMEM((2, length, step), F32),
            pltpu.VMEM((2, length, step), F32),
            pltpu.VMEM((HDIM, length), F32),
            pltpu.VMEM((length, HDIM), F32),
            pltpu.VMEM((length, HDIM), F32),
        ],
        compiler_params=pltpu.CompilerParams(vmem_limit_bytes=LIMIT),
        cost_estimate=pl.CostEstimate(
            flops=10 * length * length * 256, bytes_accessed=2200000, transcendentals=length * length
        ),
        name="spatial_attention",
    )(received)


def unpack_kernel(in_ref, dq_ref, dk_ref, dv_ref, dw_ref, full):
    low = low_lanes(HEADS * HDIM)
    values = []
    for frame in range(2):
        items = [
            in_ref[frame * HEADS + head, : HDIM + FOLD].astype(F32) for head in range(HEADS)
        ]
        both = jnp.concatenate([item[:HDIM] for item in items], axis=0).T.astype(BF16)
        dq_ref[frame] = both[:HALF]
        dk_ref[frame] = both[HALF:]
        values.append(
            jnp.concatenate(
                [
                    jnp.concatenate([item[HDIM:], swap(item[2 * FOLD :])], axis=0)
                    for item in items
                ],
                axis=0,
            )
        )
    both = jnp.where(low, values[0], swap(values[1])).T.astype(BF16)
    dv_ref[0] = both[:HALF]
    dv_ref[1] = both[HALF:]
    for s in range(2 * HEADS):
        half = 144 * (s % 2)
        unfold(
            in_ref[s].astype(F32)[HDIM + FOLD :], full, half + 8 * (s // 2), half + 128 + s // 2
        )
    dw_ref[...] = full[...].T[:288]


def unpack(received):
    shape = jax.ShapeDtypeStruct((2, HALF, HEADS * HDIM), BF16)
    return pl.pallas_call(
        unpack_kernel,
        out_shape=(shape, shape, shape, jax.ShapeDtypeStruct((288, 288), F32)),
        in_specs=vmem_specs(1),
        out_specs=tuple(vmem_specs(4)),
        scratch_shapes=[pltpu.VMEM((288, 3 * LANES), F32)],
        compiler_params=pltpu.CompilerParams(vmem_limit_bytes=LIMIT),
        name="spatial_unpack",
    )(received)


def flip(block):
    return pltpu.roll(block, HALF, 1)


def fold_tail(rest, r):
    return jnp.concatenate(
        [jnp.zeros((rest.shape[0], 32), F32), rest[:, 96 * r : 96 * r + 96]], axis=1
    )


def send_pack_kernel(
    me_ref, q_ref, k_ref, v_ref, w_ref, out0, out1, out2, out3, piece_ref, held, halves
):
    for part, ref in enumerate((q_ref, k_ref, v_ref)):
        rows = jnp.concatenate([ref[0], ref[1]], axis=0).astype(F32)
        columns = rows.T.astype(BF16)
        at = slice(part * LANES, (part + 1) * LANES)
        held[0, :, at] = columns[:288]
        held[1, :, at] = columns[288:576]
        held[2, :, at] = columns[576:864]
        held[3, :, at] = columns[864:]
    me = me_ref[0]
    for shift, out in enumerate((out0, out1, out2, out3)):
        out[...] = held[lax.rem(me + shift, 4)]

    halves[...] = jnp.zeros_like(halves)
    w = w_ref[...].astype(F32)
    halves[0, :, :288] = w[:144]
    halves[1, :, :288] = w[144:]
    core, place = me_ref[2], me_ref[1]
    block = halves[core, pl.ds(pl.multiple_of(8 * place, 8), 8)]
    rest = halves[core, 128:144]
    here = lax.broadcasted_iota(jnp.int32, rest.shape, 0) == place
    rest = jnp.sum(jnp.where(here, rest, 0.0), axis=0, keepdims=True)
    row = lax.broadcasted_iota(jnp.int32, (8, LANES), 0)
    last = block[:, 2 * LANES :]
    for r in range(3):
        last = last + jnp.where(row == r, fold_tail(rest, r), 0.0)
    piece_ref[...] = jnp.concatenate(
        [block[:, :LANES], block[:, LANES : 2 * LANES], last], axis=0
    ).astype(BF16)


def send_pack(me, q, k, v, w):
    shape = jax.ShapeDtypeStruct((288, 3 * LANES), BF16)
    piece = jax.ShapeDtypeStruct((24, LANES), BF16)
    return pl.pallas_call(
        send_pack_kernel,
        out_shape=(shape,) * 4 + (piece,),
        in_specs=[pl.BlockSpec(memory_space=pltpu.SMEM)] + vmem_specs(4),
        out_specs=tuple(vmem_specs(5)),
        scratch_shapes=[
            pltpu.VMEM((4, 288, 3 * LANES), BF16),
            pltpu.VMEM((2, 144, 3 * LANES), F32),
        ],
        compiler_params=pltpu.CompilerParams(vmem_limit_bytes=LIMIT),
        name="temporal_pack",
    )(me, q, k, v, w)


def rows_of(values):
    return jnp.concatenate([jnp.sum(value, axis=0, keepdims=True) for value in values], axis=0)


def frame_weights(query, keys):
    scores = rows_of([query * key for key in keys])
    peak = jnp.max(scores, axis=0, keepdims=True)
    raised = jnp.exp2((scores - peak) * (math.log2(math.e) / math.sqrt(HDIM)))
    return raised / jnp.sum(raised, axis=0, keepdims=True)


def rounded(value):
    return value.astype(BF16).astype(F32)


def head_rows(wide, head, part):
    rows = pl.ds(pl.multiple_of(head * HDIM, 8), HDIM)
    at = slice(part * LANES, (part + 1) * LANES)
    return [wide[shift, rows, at] for shift in range(4)]


def both_ways(blocks):
    out = []
    for block in blocks:
        out += [block, flip(block)]
    return out


def tout_kernel(me_ref, in0, in1, in2, in3, out_ref, wide, total):
    for shift, ref in enumerate((in0, in1, in2, in3)):
        wide[shift] = ref[...].astype(F32)

    def body(head, _):
        queries = head_rows(wide, head, 0)
        keys = both_ways(head_rows(wide, head, 1))
        values = both_ways(head_rows(wide, head, 2))
        for shift in range(4):
            weights = rounded(frame_weights(queries[shift], keys))
            out = weights[0:1] * values[0]
            for j in range(1, 8):
                out = out + weights[j : j + 1] * values[j]
            total[shift, pl.ds(pl.multiple_of(head * HDIM, 8), HDIM)] = out
        return 0

    lax.fori_loop(0, 4, body, 0)
    me = me_ref[0]
    for shift in range(4):
        out_ref[lax.rem(me + 4 - shift, 4)] = total[shift].astype(BF16)


def temporal_out(me, pieces):
    return pl.pallas_call(
        tout_kernel,
        out_shape=jax.ShapeDtypeStruct((4, 288, LANES), BF16),
        in_specs=[pl.BlockSpec(memory_space=pltpu.SMEM)] + vmem_specs(4),
        out_specs=pl.BlockSpec(memory_space=pltpu.VMEM),
        scratch_shapes=[
            pltpu.VMEM((4, 288, 3 * LANES), F32),
            pltpu.VMEM((4, 288, LANES), F32),
        ],
        compiler_params=pltpu.CompilerParams(vmem_limit_bytes=LIMIT),
        name="temporal_tout",
    )(me, *pieces)


def partial_kernel(me_ref, tout_ref, grad_ref, keep_ref, send_ref, full, *, scale):
    total = jnp.dot(tout_ref[0], grad_ref[0], preferred_element_type=F32)
    for a in range(1, 4):
        total = total + jnp.dot(tout_ref[a], grad_ref[a], preferred_element_type=F32)
    total = total * scale
    full[0] = total[:144]
    full[1] = total[144:]
    core = me_ref[2]
    keep_ref[...] = full[core]
    send_ref[...] = full[1 - core].astype(BF16)


def weight_partial(me, tout, grads, scale):
    return pl.pallas_call(
        functools.partial(partial_kernel, scale=scale),
        out_shape=(
            jax.ShapeDtypeStruct((144, 1152), F32),
            jax.ShapeDtypeStruct((144, 1152), BF16),
        ),
        in_specs=[pl.BlockSpec(memory_space=pltpu.SMEM)] + vmem_specs(2),
        out_specs=tuple(vmem_specs(2)),
        scratch_shapes=[pltpu.VMEM((2, 144, 1152), F32)],
        compiler_params=pltpu.CompilerParams(vmem_limit_bytes=LIMIT),
        name="weight_partial",
    )(me, tout, grads)


def weight_split_kernel(keep_ref, got_ref, piece_ref, out_ref, full, part):
    full[...] = keep_ref[...] + got_ref[...].astype(F32)
    part[...] = jnp.zeros_like(part)
    row = lax.broadcasted_iota(jnp.int32, (16, 8, LANES), 1)
    copies = jnp.broadcast_to(piece_ref[...].astype(F32)[None], (16, 24, LANES))
    for d in range(4):
        part[:, :288] = full[:, d * 288 : (d + 1) * 288]
        tiles = [
            part[:128, tile * LANES : (tile + 1) * LANES].reshape(16, 8, LANES)
            for tile in range(3)
        ]
        rest = part[128:144, :]
        for r in range(3):
            tiles[2] = tiles[2] + jnp.where(row == r, fold_tail(rest, r)[:, None, :], 0.0)
        out_ref[d * 16 : (d + 1) * 16] = jnp.concatenate(tiles + [copies], axis=1).astype(BF16)


def weight_split(keep, got, piece):
    return pl.pallas_call(
        weight_split_kernel,
        out_shape=jax.ShapeDtypeStruct((64, 48, LANES), BF16),
        in_specs=vmem_specs(3),
        out_specs=pl.BlockSpec(memory_space=pltpu.VMEM),
        scratch_shapes=[pltpu.VMEM((144, 1152), F32), pltpu.VMEM((144, 3 * LANES), F32)],
        compiler_params=pltpu.CompilerParams(vmem_limit_bytes=LIMIT),
        name="weight_split",
    )(keep, got, piece)


def unfold(block, full, start, last):
    for tile in range(3):
        at = slice(tile * LANES, (tile + 1) * LANES)
        full[start : start + 8, at] = block[tile * 8 : tile * 8 + 8]
    for r in range(3):
        full[last : last + 1, 96 * r : 96 * r + 96] = block[16 + r : 17 + r, 32:]


def weight_join_kernel(spatial_ref, in_ref, out_ref, w_ref, full):
    total = None
    for s in range(64):
        block = in_ref[s].astype(F32)
        total = block[:24] if total is None else total + block[:24]
        d, j = s // 16, s % 16
        unfold(block[24:], full, d * 144 + 8 * j, d * 144 + 128 + j)
    copy = total.astype(BF16)
    for s in range(32):
        out_ref[s, : HDIM + FOLD] = spatial_ref[s]
        out_ref[s, HDIM + FOLD :] = copy
    for d in range(4):
        w_ref[d] = full[d * 144 : (d + 1) * 144, :288].astype(BF16)


def weight_join(spatial, received):
    return pl.pallas_call(
        weight_join_kernel,
        out_shape=(
            jax.ShapeDtypeStruct((32, HDIM + FOLD + 24, LANES), BF16),
            jax.ShapeDtypeStruct((4, 144, 288), BF16),
        ),
        in_specs=vmem_specs(2),
        out_specs=tuple(vmem_specs(2)),
        scratch_shapes=[pltpu.VMEM((576, 3 * LANES), F32)],
        compiler_params=pltpu.CompilerParams(vmem_limit_bytes=LIMIT),
        name="weight_join",
    )(spatial, received)


def temporal_kernel(
    me_ref, in0, in1, in2, in3, grad_ref, own_ref, other_ref,
    out0, out1, out2, out3, wide, back, halves,
):
    me, core = me_ref[0], me_ref[2]
    for d in range(4):
        halves[2 * d + core] = own_ref[d]
        halves[2 * d + 1 - core] = other_ref[d]
    w = halves[...].reshape(1152, 288)
    for shift, ref in enumerate((in0, in1, in2, in3)):
        wide[shift, :, : 3 * LANES] = ref[...].astype(F32)
        grads = grad_ref[lax.rem(me + 4 - shift, 4)]
        tgrad = rounded(jnp.dot(grads, w, preferred_element_type=F32))
        wide[shift, :, 3 * LANES :] = tgrad.T
    scale = 1.0 / math.sqrt(HDIM)

    def body(head, _):
        rows = pl.ds(pl.multiple_of(head * HDIM, 8), HDIM)
        queries = head_rows(wide, head, 0)
        keys = both_ways(head_rows(wide, head, 1))
        values = both_ways(head_rows(wide, head, 2))
        grads = head_rows(wide, head, 3)
        low_w, low_s = [], []
        for shift in range(4):
            weights = frame_weights(queries[shift], keys)
            pgrad = rows_of([grads[shift] * value for value in values])
            inner = jnp.sum(weights * pgrad, axis=0, keepdims=True)
            low_w.append(rounded(weights))
            low_s.append(rounded(weights * (pgrad - inner)))
            dq = low_s[shift][0:1] * keys[0]
            for j in range(1, 8):
                dq = dq + low_s[shift][j : j + 1] * keys[j]
            back[shift, rows, 0:LANES] = dq * scale
        for b in range(4):
            for part, (coefs, terms, factor) in enumerate(
                ((low_s, queries, scale), (low_w, grads, 1.0)), 1
            ):
                sums = []
                for way in range(2):
                    j = 2 * b + way
                    total = coefs[0][j : j + 1] * terms[0]
                    for shift in range(1, 4):
                        total = total + coefs[shift][j : j + 1] * terms[shift]
                    sums.append(total)
                back[b, rows, part * LANES : (part + 1) * LANES] = (
                    sums[0] + flip(sums[1])
                ) * factor
        return 0

    lax.fori_loop(0, 4, body, 0)
    for shift, out in enumerate((out0, out1, out2, out3)):
        out[...] = back[shift].astype(BF16)


def temporal_back(me, pieces, grads, own, other):
    shape = jax.ShapeDtypeStruct((288, 3 * LANES), BF16)
    return pl.pallas_call(
        temporal_kernel,
        out_shape=(shape,) * 4,
        in_specs=[pl.BlockSpec(memory_space=pltpu.SMEM)] + vmem_specs(7),
        out_specs=tuple(vmem_specs(4)),
        scratch_shapes=[
            pltpu.VMEM((4, 288, 4 * LANES), F32),
            pltpu.VMEM((4, 288, 3 * LANES), F32),
            pltpu.VMEM((8, 144, 288), BF16),
        ],
        compiler_params=pltpu.CompilerParams(vmem_limit_bytes=LIMIT),
        name="temporal_back",
    )(me, *pieces, grads, own, other)


def receive_kernel(me_ref, in0, in1, in2, in3, dq_ref, dk_ref, dv_ref, held):
    me = me_ref[0]
    for shift, ref in enumerate((in0, in1, in2, in3)):
        held[lax.rem(me + shift, 4)] = ref[...]
    for part, out in enumerate((dq_ref, dk_ref, dv_ref)):
        at = slice(part * LANES, (part + 1) * LANES)
        columns = jnp.concatenate([held[t, :, at] for t in range(4)], axis=0).astype(F32)
        rows = columns.T.astype(BF16)
        out[0] = rows[:HALF]
        out[1] = rows[HALF:]


def receive(me, pieces):
    shape = jax.ShapeDtypeStruct((2, HALF, HEADS * HDIM), BF16)
    return pl.pallas_call(
        receive_kernel,
        out_shape=(shape,) * 3,
        in_specs=[pl.BlockSpec(memory_space=pltpu.SMEM)] + vmem_specs(4),
        out_specs=tuple(vmem_specs(3)),
        scratch_shapes=[pltpu.VMEM((4, 288, 3 * LANES), BF16)],
        compiler_params=pltpu.CompilerParams(vmem_limit_bytes=LIMIT),
        name="temporal_unpack",
    )(me, *pieces)


SWAP_CORE = [(0, 1), (1, 0)]
RING = [[(i, (i + s) % 4) for i in range(4)] for s in (1, 2, 3)]
RING_BACK = [[(i, (i - s) % 4) for i in range(4)] for s in (1, 2, 3)]


def shards(
    q_spatial,
    k_spatial,
    v_spatial,
    grad_spatial,
    q_temporal,
    k_temporal,
    v_temporal,
    grad_out,
    w_tout,
):
    me = jnp.stack(
        [lax.axis_index("tm"), 4 * lax.axis_index("z") + lax.axis_index("y"), lax.axis_index("c")]
    )
    space = ("z", "y", "c")
    grads = lax.all_gather(grad_out, "tm", axis=1, tiled=True).reshape(4, LANES, 1152)
    packed = pack(q_spatial[0], k_spatial[0], v_spatial[0], grad_spatial[0])
    packed, q, k, v = lax.optimization_barrier(
        (packed, q_temporal[0], k_temporal[0], v_temporal[0])
    )
    received = lax.all_to_all(packed, space, split_axis=0, concat_axis=0, tiled=True)

    *sends, piece = send_pack(me, q, k, v, w_tout)
    pieces = (sends[0],) + tuple(
        lax.ppermute(sends[shift], "tm", RING[shift - 1]) for shift in (1, 2, 3)
    )
    tout = temporal_out(me, pieces)
    keep, send = weight_partial(me, tout, grads, 1.0 / math.sqrt(65536))
    blocks = weight_split(keep, lax.ppermute(send, "c", SWAP_CORE), piece)

    received, blocks = lax.optimization_barrier((received, blocks))
    blocks = lax.all_to_all(blocks, ("dp", "z", "y"), split_axis=0, concat_axis=0, tiled=True)
    results, own = weight_join(attend(received), blocks)
    returned = lax.all_to_all(results, space, split_axis=0, concat_axis=0, tiled=True)

    backs = temporal_back(me, pieces, grads, own, lax.ppermute(own, "c", SWAP_CORE))
    homes = (backs[0],) + tuple(
        lax.ppermute(backs[shift], "tm", RING_BACK[shift - 1]) for shift in (1, 2, 3)
    )
    dq_t, dk_t, dv_t = receive(me, homes)
    dq, dk, dv, weight_grad = unpack(returned)
    return (dq[None], dk[None], dv[None], dq_t[None], dk_t[None], dv_t[None], weight_grad)


def solution(mesh):
    sizes = (mesh.shape["dp"], mesh.shape["tm"], 4, 4, 2)
    split = jax.sharding.Mesh(mesh.devices.reshape(sizes), ("dp", "tm", "z", "y", "c"))
    field = P("dp", "tm", ("z", "y", "c"), None)
    return jax.shard_map(
        shards,
        mesh=split,
        in_specs=(field,) * 8 + (P("dp", "tm"),),
        out_specs=(field,) * 6 + (P("dp", "tm"),),
        check_vma=False,
    )
```

```python
import math
import functools
import jax
import jax.numpy as jnp
from jax import lax
from jax.experimental import pallas as pl
from jax.experimental.pallas import tpu as pltpu
from jax.sharding import PartitionSpec as P

HEADS = 16
HDIM = 72
LANES = 128
HALF = 64
FOLD = 40
F32 = jnp.float32
BF16 = jnp.bfloat16
LIMIT = 56 * 1024 * 1024
SMALL = pl.CostEstimate(flops=1000, bytes_accessed=1000, transcendentals=0)


def vmem_specs(count):
    return [pl.BlockSpec(memory_space=pltpu.VMEM)] * count


def low_lanes(rows):
    return lax.broadcasted_iota(jnp.int32, (rows, LANES), 1) < HALF


def swap(block):
    return pltpu.roll(block, HALF, 1)


def pack_kernel(q_ref, k_ref, v_ref, g_ref, out_ref):
    for frame in range(2):
        for pair, (first, second) in enumerate(((q_ref, k_ref), (v_ref, g_ref))):
            rows = jnp.concatenate([first[frame], second[frame]], axis=0).astype(F32)
            columns = rows.T
            for head in range(HEADS):
                out_ref[frame * HEADS + head, pair] = columns[
                    head * HDIM : (head + 1) * HDIM
                ].astype(BF16)


def pack(q, k, v, g):
    return pl.pallas_call(
        pack_kernel,
        out_shape=jax.ShapeDtypeStruct((2 * HEADS, 2, HDIM, LANES), BF16),
        in_specs=vmem_specs(4),
        out_specs=pl.BlockSpec(memory_space=pltpu.VMEM),
        compiler_params=pltpu.CompilerParams(vmem_limit_bytes=LIMIT),
        cost_estimate=SMALL,
        name="spatial_pack",
    )(q, k, v, g)


def attend_kernel(
    in_ref, out_ref, q_t, k_t, g_t, q_n, k_n, v_n, g_n, s_buf, p_buf, dq_t, dk_n, dv_n, *, step
):
    length = q_t.shape[1]
    pairs = length // LANES
    scale = 1.0 / math.sqrt(HDIM)
    power = scale * math.log2(math.e)

    def split(j, pair):
        first = in_ref[2 * j, pair].astype(F32)
        second = in_ref[2 * j + 1, pair].astype(F32)
        low = low_lanes(HDIM)
        return (
            jnp.where(low, first, swap(second)),
            jnp.where(low, swap(first), second),
        )

    for j in range(pairs):
        at = slice(j * LANES, (j + 1) * LANES)
        q, k = split(j, 0)
        v, g = split(j, 1)
        q_t[:, at] = q.astype(BF16)
        k_t[:, at] = k.astype(BF16)
        g_t[:, at] = g.astype(BF16)
        q_n[at, :] = q.T.astype(BF16)
        k_n[at, :] = k.T.astype(BF16)
        v_n[at, :] = v.T.astype(BF16)
        g_n[at, :] = g.T.astype(BF16)

    blocks = length // step

    def products(i, slot):
        at = pl.ds(pl.multiple_of(i * step, step), step)
        s_buf[slot] = jnp.dot(k_n[...], q_t[:, at], preferred_element_type=F32)
        p_buf[slot] = jnp.dot(v_n[...], g_t[:, at], preferred_element_type=F32)

    def rest(i, slot, first):
        at = pl.ds(pl.multiple_of(i * step, step), step)
        scores = s_buf[slot]
        peak = jnp.max(scores, axis=0, keepdims=True)
        raised = jnp.exp2((scores - peak) * power)
        over = 1.0 / jnp.sum(raised, axis=0, keepdims=True)
        grads = p_buf[slot]
        inner = jnp.sum(raised * grads, axis=0, keepdims=True) * over
        weights = raised * over
        low_w = weights.astype(BF16)
        low_s = (weights * (grads - inner)).astype(BF16)
        dv = jnp.dot(low_w, g_n[at, :], preferred_element_type=F32)
        dk = jnp.dot(low_s, q_n[at, :], preferred_element_type=F32)
        if first:
            dv_n[...] = dv
            dk_n[...] = dk
        else:
            dv_n[...] += dv
            dk_n[...] += dk
        dq_t[:, at] = jnp.dot(k_t[...], low_s, preferred_element_type=F32) * scale

    products(0, 0)
    products(1, 1)
    rest(0, 0, True)

    def body(i, _):
        slot = lax.rem(i, 2)
        products(i + 1, 1 - slot)
        rest(i, slot, False)
        return 0

    lax.fori_loop(1, blocks - 1, body, 0)
    rest(blocks - 1, (blocks - 1) % 2, False)

    for j in range(pairs):
        at = slice(j * LANES, (j + 1) * LANES)
        dq = dq_t[:, at]
        dk = (dk_n[at, :] * scale).T
        dv = dv_n[at, :].T
        low = low_lanes(HDIM)
        low_f = low_lanes(FOLD)
        upper, lower = dv[:FOLD], dv[HDIM - FOLD :]
        out_ref[2 * j] = jnp.concatenate(
            [jnp.where(low, dq, swap(dk)), jnp.where(low_f, upper, swap(lower))], axis=0
        ).astype(BF16)
        out_ref[2 * j + 1] = jnp.concatenate(
            [jnp.where(low, swap(dq), dk), jnp.where(low_f, swap(upper), lower)], axis=0
        ).astype(BF16)


def attend(received, step=256):
    sources = received.shape[0]
    length = sources * HALF
    wide = pltpu.VMEM((HDIM, length), BF16)
    tall = pltpu.VMEM((length, HDIM), BF16)
    return pl.pallas_call(
        functools.partial(attend_kernel, step=step),
        out_shape=jax.ShapeDtypeStruct((sources, HDIM + FOLD, LANES), BF16),
        in_specs=vmem_specs(1),
        out_specs=pl.BlockSpec(memory_space=pltpu.VMEM),
        scratch_shapes=[
            wide, wide, wide, tall, tall, tall, tall,
            pltpu.VMEM((2, length, step), F32),
            pltpu.VMEM((2, length, step), F32),
            pltpu.VMEM((HDIM, length), F32),
            pltpu.VMEM((length, HDIM), F32),
            pltpu.VMEM((length, HDIM), F32),
        ],
        compiler_params=pltpu.CompilerParams(vmem_limit_bytes=LIMIT),
        cost_estimate=pl.CostEstimate(
            flops=10 * length * length * 256, bytes_accessed=2200000, transcendentals=length * length
        ),
        name="spatial_attention",
    )(received)


def unpack_kernel(in_ref, dq_ref, dk_ref, dv_ref, dw_ref, full):
    low = low_lanes(HEADS * HDIM)
    values = []
    for frame in range(2):
        items = [
            in_ref[frame * HEADS + head, : HDIM + FOLD].astype(F32) for head in range(HEADS)
        ]
        both = jnp.concatenate([item[:HDIM] for item in items], axis=0).T.astype(BF16)
        dq_ref[frame] = both[:HALF]
        dk_ref[frame] = both[HALF:]
        values.append(
            jnp.concatenate(
                [
                    jnp.concatenate([item[HDIM:], swap(item[2 * FOLD :])], axis=0)
                    for item in items
                ],
                axis=0,
            )
        )
    both = jnp.where(low, values[0], swap(values[1])).T.astype(BF16)
    dv_ref[0] = both[:HALF]
    dv_ref[1] = both[HALF:]
    for s in range(2 * HEADS):
        half = 144 * (s % 2)
        unfold(
            in_ref[s].astype(F32)[HDIM + FOLD :], full, half + 8 * (s // 2), half + 128 + s // 2
        )
    dw_ref[...] = full[...].T[:288]


def unpack(received):
    shape = jax.ShapeDtypeStruct((2, HALF, HEADS * HDIM), BF16)
    return pl.pallas_call(
        unpack_kernel,
        out_shape=(shape, shape, shape, jax.ShapeDtypeStruct((288, 288), F32)),
        in_specs=vmem_specs(1),
        out_specs=tuple(vmem_specs(4)),
        scratch_shapes=[pltpu.VMEM((288, 3 * LANES), F32)],
        compiler_params=pltpu.CompilerParams(vmem_limit_bytes=LIMIT),
        name="spatial_unpack",
    )(received)


def flip(block):
    return pltpu.roll(block, HALF, 1)


def fold_tail(rest, r):
    return jnp.concatenate(
        [jnp.zeros((rest.shape[0], 32), F32), rest[:, 96 * r : 96 * r + 96]], axis=1
    )


def send_pack_kernel(me_ref, q_ref, k_ref, v_ref, out0, out1, out2, out3, held):
    for part, ref in enumerate((q_ref, k_ref, v_ref)):
        rows = jnp.concatenate([ref[0], ref[1]], axis=0).astype(F32)
        columns = rows.T.astype(BF16)
        at = slice(part * LANES, (part + 1) * LANES)
        held[0, :, at] = columns[:288]
        held[1, :, at] = columns[288:576]
        held[2, :, at] = columns[576:864]
        held[3, :, at] = columns[864:]
    me = me_ref[0]
    for shift, out in enumerate((out0, out1, out2, out3)):
        out[...] = held[lax.rem(me + shift, 4)]


def send_pack(me, q, k, v):
    shape = jax.ShapeDtypeStruct((288, 3 * LANES), BF16)
    return pl.pallas_call(
        send_pack_kernel,
        out_shape=(shape,) * 4,
        in_specs=[pl.BlockSpec(memory_space=pltpu.SMEM)] + vmem_specs(3),
        out_specs=tuple(vmem_specs(4)),
        scratch_shapes=[pltpu.VMEM((4, 288, 3 * LANES), BF16)],
        compiler_params=pltpu.CompilerParams(vmem_limit_bytes=LIMIT),
        cost_estimate=SMALL,
        name="temporal_pack",
    )(me, q, k, v)


def rows_of(values):
    return jnp.concatenate([jnp.sum(value, axis=0, keepdims=True) for value in values], axis=0)


def frame_weights(query, keys):
    scores = rows_of([query * key for key in keys])
    peak = jnp.max(scores, axis=0, keepdims=True)
    raised = jnp.exp2((scores - peak) * (math.log2(math.e) / math.sqrt(HDIM)))
    return raised / jnp.sum(raised, axis=0, keepdims=True)


def rounded(value):
    return value.astype(BF16).astype(F32)


def head_rows(wide, head, part):
    rows = pl.ds(pl.multiple_of(head * HDIM, 8), HDIM)
    at = slice(part * LANES, (part + 1) * LANES)
    return [wide[shift, rows, at] for shift in range(4)]


def both_ways(blocks):
    out = []
    for block in blocks:
        out += [block, flip(block)]
    return out


def tout_kernel(me_ref, in0, in1, in2, in3, out_ref, wide, total):
    for shift, ref in enumerate((in0, in1, in2, in3)):
        wide[shift] = ref[...].astype(F32)

    def body(head, _):
        queries = head_rows(wide, head, 0)
        keys = both_ways(head_rows(wide, head, 1))
        values = both_ways(head_rows(wide, head, 2))
        for shift in range(4):
            weights = rounded(frame_weights(queries[shift], keys))
            out = weights[0:1] * values[0]
            for j in range(1, 8):
                out = out + weights[j : j + 1] * values[j]
            total[shift, pl.ds(pl.multiple_of(head * HDIM, 8), HDIM)] = out
        return 0

    lax.fori_loop(0, 4, body, 0)
    me = me_ref[0]
    for shift in range(4):
        out_ref[lax.rem(me + 4 - shift, 4)] = total[shift].astype(BF16)


def temporal_out(me, pieces):
    return pl.pallas_call(
        tout_kernel,
        out_shape=jax.ShapeDtypeStruct((4, 288, LANES), BF16),
        in_specs=[pl.BlockSpec(memory_space=pltpu.SMEM)] + vmem_specs(4),
        out_specs=pl.BlockSpec(memory_space=pltpu.VMEM),
        scratch_shapes=[
            pltpu.VMEM((4, 288, 3 * LANES), F32),
            pltpu.VMEM((4, 288, LANES), F32),
        ],
        compiler_params=pltpu.CompilerParams(vmem_limit_bytes=LIMIT),
        cost_estimate=SMALL,
        name="temporal_tout",
    )(me, *pieces)


def partial_kernel(
    me_ref, tout_ref, grad_ref, w_ref, keep_ref, send_ref, slice_ref, full, stage, rows, *, scale
):
    total = jnp.dot(tout_ref[0], grad_ref[0], preferred_element_type=F32)
    for a in range(1, 4):
        total = total + jnp.dot(tout_ref[a], grad_ref[a], preferred_element_type=F32)
    total = total * scale
    full[0] = total[:144]
    full[1] = total[144:]
    core, eighth = me_ref[2], me_ref[1]
    keep_ref[...] = full[core]
    send_ref[...] = full[1 - core].astype(BF16)

    rows[...] = w_ref[...].astype(F32)
    stage[...] = jnp.zeros_like(stage)
    tail = rows[256:288]
    index = lax.broadcasted_iota(jnp.int32, tail.shape, 0)
    for k in range(4):
        at = slice(288 * k, 288 * (k + 1))
        stage[0:8, at] = rows[pl.ds(pl.multiple_of(32 * eighth + 8 * k, 8), 8)]
        stage[8:9, at] = jnp.sum(
            jnp.where(index == 4 * eighth + k, tail, 0.0), axis=0, keepdims=True
        )
    slice_ref[...] = stage[...].astype(BF16)


def weight_partial(me, tout, grads, w, scale):
    return pl.pallas_call(
        functools.partial(partial_kernel, scale=scale),
        out_shape=(
            jax.ShapeDtypeStruct((144, 1152), F32),
            jax.ShapeDtypeStruct((144, 1152), BF16),
            jax.ShapeDtypeStruct((16, 1152), BF16),
        ),
        in_specs=[pl.BlockSpec(memory_space=pltpu.SMEM)] + vmem_specs(3),
        out_specs=tuple(vmem_specs(3)),
        scratch_shapes=[
            pltpu.VMEM((2, 144, 1152), F32),
            pltpu.VMEM((16, 1152), F32),
            pltpu.VMEM((288, 288), F32),
        ],
        compiler_params=pltpu.CompilerParams(vmem_limit_bytes=LIMIT),
        name="weight_partial",
    )(me, tout, grads, w)


def weight_split_kernel(keep_ref, got_ref, out_ref, full, part):
    full[...] = keep_ref[...] + got_ref[...].astype(F32)
    part[...] = jnp.zeros_like(part)
    row = lax.broadcasted_iota(jnp.int32, (16, 8, LANES), 1)
    for d in range(4):
        part[:, :288] = full[:, d * 288 : (d + 1) * 288]
        tiles = [
            part[:128, tile * LANES : (tile + 1) * LANES].reshape(16, 8, LANES)
            for tile in range(3)
        ]
        rest = part[128:144, :]
        for r in range(3):
            tiles[2] = tiles[2] + jnp.where(row == r, fold_tail(rest, r)[:, None, :], 0.0)
        out_ref[d * 16 : (d + 1) * 16] = jnp.concatenate(tiles, axis=1).astype(BF16)


def fold_tail(rest, r):
    return jnp.concatenate(
        [jnp.zeros((rest.shape[0], 32), F32), rest[:, 96 * r : 96 * r + 96]], axis=1
    )


def weight_split(keep, got):
    return pl.pallas_call(
        weight_split_kernel,
        out_shape=jax.ShapeDtypeStruct((64, 24, LANES), BF16),
        in_specs=vmem_specs(2),
        out_specs=pl.BlockSpec(memory_space=pltpu.VMEM),
        scratch_shapes=[pltpu.VMEM((144, 1152), F32), pltpu.VMEM((144, 3 * LANES), F32)],
        compiler_params=pltpu.CompilerParams(vmem_limit_bytes=LIMIT),
        name="weight_split",
    )(keep, got)


def unfold(block, full, start, last):
    for tile in range(3):
        at = slice(tile * LANES, (tile + 1) * LANES)
        full[start : start + 8, at] = block[tile * 8 : tile * 8 + 8]
    for r in range(3):
        full[last : last + 1, 96 * r : 96 * r + 96] = block[16 + r : 17 + r, 32:]


def weight_join_kernel(spatial_ref, in_ref, out_ref):
    total = in_ref[0].astype(F32)
    for s in range(1, 64):
        total = total + in_ref[s].astype(F32)
    copy = total.astype(BF16)
    for s in range(32):
        out_ref[s, : HDIM + FOLD] = spatial_ref[s]
        out_ref[s, HDIM + FOLD :] = copy


def weight_join(spatial, received):
    return pl.pallas_call(
        weight_join_kernel,
        out_shape=jax.ShapeDtypeStruct((32, HDIM + FOLD + 24, LANES), BF16),
        in_specs=vmem_specs(2),
        out_specs=pl.BlockSpec(memory_space=pltpu.VMEM),
        compiler_params=pltpu.CompilerParams(vmem_limit_bytes=LIMIT),
        name="weight_join",
    )(spatial, received)


def temporal_kernel(
    me_ref, in0, in1, in2, in3, grad_ref, w_ref, out0, out1, out2, out3, wide, back, full
):
    me = me_ref[0]
    for d in range(4):
        for y in range(4):
            for c in range(2):
                block = w_ref[d * 8 + y * 2 + c].astype(F32)
                eighth = 4 * c + y
                for k in range(4):
                    at = slice(288 * k, 288 * (k + 1))
                    start = d * 288 + 32 * eighth + 8 * k
                    full[start : start + 8] = block[0:8, at]
                    start = d * 288 + 256 + 4 * eighth + k
                    full[start : start + 1] = block[8:9, at]
    w = full[...].astype(BF16)
    for shift, ref in enumerate((in0, in1, in2, in3)):
        wide[shift, :, : 3 * LANES] = ref[...].astype(F32)
        grads = grad_ref[lax.rem(me + 4 - shift, 4)]
        tgrad = rounded(jnp.dot(grads, w, preferred_element_type=F32))
        wide[shift, :, 3 * LANES :] = tgrad.T
    scale = 1.0 / math.sqrt(HDIM)

    def body(head, _):
        rows = pl.ds(pl.multiple_of(head * HDIM, 8), HDIM)
        queries = head_rows(wide, head, 0)
        keys = both_ways(head_rows(wide, head, 1))
        values = both_ways(head_rows(wide, head, 2))
        grads = head_rows(wide, head, 3)
        low_w, low_s = [], []
        for shift in range(4):
            weights = frame_weights(queries[shift], keys)
            pgrad = rows_of([grads[shift] * value for value in values])
            inner = jnp.sum(weights * pgrad, axis=0, keepdims=True)
            low_w.append(rounded(weights))
            low_s.append(rounded(weights * (pgrad - inner)))
            dq = low_s[shift][0:1] * keys[0]
            for j in range(1, 8):
                dq = dq + low_s[shift][j : j + 1] * keys[j]
            back[shift, rows, 0:LANES] = dq * scale
        for b in range(4):
            for part, (coefs, terms, factor) in enumerate(
                ((low_s, queries, scale), (low_w, grads, 1.0)), 1
            ):
                sums = []
                for way in range(2):
                    j = 2 * b + way
                    total = coefs[0][j : j + 1] * terms[0]
                    for shift in range(1, 4):
                        total = total + coefs[shift][j : j + 1] * terms[shift]
                    sums.append(total)
                back[b, rows, part * LANES : (part + 1) * LANES] = (
                    sums[0] + flip(sums[1])
                ) * factor
        return 0

    lax.fori_loop(0, 4, body, 0)
    for shift, out in enumerate((out0, out1, out2, out3)):
        out[...] = back[shift].astype(BF16)


def temporal_back(me, pieces, grads, w):
    shape = jax.ShapeDtypeStruct((288, 3 * LANES), BF16)
    return pl.pallas_call(
        temporal_kernel,
        out_shape=(shape,) * 4,
        in_specs=[pl.BlockSpec(memory_space=pltpu.SMEM)] + vmem_specs(6),
        out_specs=tuple(vmem_specs(4)),
        scratch_shapes=[
            pltpu.VMEM((4, 288, 4 * LANES), F32),
            pltpu.VMEM((4, 288, 3 * LANES), F32),
            pltpu.VMEM((1152, 288), F32),
        ],
        compiler_params=pltpu.CompilerParams(vmem_limit_bytes=LIMIT),
        name="temporal_back",
    )(me, *pieces, grads, w)


def receive_kernel(me_ref, in0, in1, in2, in3, dq_ref, dk_ref, dv_ref, held):
    me = me_ref[0]
    for shift, ref in enumerate((in0, in1, in2, in3)):
        held[lax.rem(me + shift, 4)] = ref[...]
    for part, out in enumerate((dq_ref, dk_ref, dv_ref)):
        at = slice(part * LANES, (part + 1) * LANES)
        columns = jnp.concatenate([held[t, :, at] for t in range(4)], axis=0).astype(F32)
        rows = columns.T.astype(BF16)
        out[0] = rows[:HALF]
        out[1] = rows[HALF:]


def receive(me, pieces):
    shape = jax.ShapeDtypeStruct((2, HALF, HEADS * HDIM), BF16)
    return pl.pallas_call(
        receive_kernel,
        out_shape=(shape,) * 3,
        in_specs=[pl.BlockSpec(memory_space=pltpu.SMEM)] + vmem_specs(4),
        out_specs=tuple(vmem_specs(3)),
        scratch_shapes=[pltpu.VMEM((4, 288, 3 * LANES), BF16)],
        compiler_params=pltpu.CompilerParams(vmem_limit_bytes=LIMIT),
        name="temporal_unpack",
    )(me, *pieces)


SWAP_CORE = [(0, 1), (1, 0)]
RING = [[(i, (i + s) % 4) for i in range(4)] for s in (1, 2, 3)]
RING_BACK = [[(i, (i - s) % 4) for i in range(4)] for s in (1, 2, 3)]


def shards(
    q_spatial,
    k_spatial,
    v_spatial,
    grad_spatial,
    q_temporal,
    k_temporal,
    v_temporal,
    grad_out,
    w_tout,
):
    core = lax.axis_index("c")
    me = jnp.stack([lax.axis_index("tm"), 4 * core + lax.axis_index("y"), core])
    space = ("z", "y", "c")
    grads = lax.all_gather(grad_out, "tm", axis=1, tiled=True).reshape(4, LANES, 1152)
    packed = pack(q_spatial[0], k_spatial[0], v_spatial[0], grad_spatial[0])
    packed, q, k, v = lax.optimization_barrier(
        (packed, q_temporal[0], k_temporal[0], v_temporal[0])
    )
    received = lax.all_to_all(packed, space, split_axis=0, concat_axis=0, tiled=True)

    sends = send_pack(me, q, k, v)
    pieces = (sends[0],) + tuple(
        lax.ppermute(sends[shift], "tm", RING[shift - 1]) for shift in (1, 2, 3)
    )
    tout = temporal_out(me, pieces)
    keep, send, eighth = weight_partial(me, tout, grads, w_tout, 1.0 / math.sqrt(65536))
    weight = lax.all_gather(eighth, ("dp", "y", "c"), axis=0, tiled=True).reshape(32, 16, 1152)
    blocks = weight_split(keep, lax.ppermute(send, "c", SWAP_CORE))

    received, blocks = lax.optimization_barrier((received, blocks))
    blocks = lax.all_to_all(blocks, ("dp", "z", "y"), split_axis=0, concat_axis=0, tiled=True)
    results = weight_join(attend(received), blocks)
    results, *pieces = lax.optimization_barrier((results,) + pieces)
    returned = lax.all_to_all(results, space, split_axis=0, concat_axis=0, tiled=True)

    backs = temporal_back(me, pieces, grads, weight)
    homes = (backs[0],) + tuple(
        lax.ppermute(backs[shift], "tm", RING_BACK[shift - 1]) for shift in (1, 2, 3)
    )
    dq_t, dk_t, dv_t = receive(me, homes)
    dq, dk, dv, weight_grad = unpack(returned)
    return (dq[None], dk[None], dv[None], dq_t[None], dk_t[None], dv_t[None], weight_grad)


def solution(mesh):
    sizes = (mesh.shape["dp"], mesh.shape["tm"], 4, 4, 2)
    split = jax.sharding.Mesh(mesh.devices.reshape(sizes), ("dp", "tm", "z", "y", "c"))
    field = P("dp", "tm", ("z", "y", "c"), None)
    return jax.shard_map(
        shards,
        mesh=split,
        in_specs=(field,) * 8 + (P("dp", "tm"),),
        out_specs=(field,) * 6 + (P("dp", "tm"),),
        check_vma=False,
    )
```

```python
import math
import functools
import jax
import jax.numpy as jnp
from jax import lax
from jax.experimental import pallas as pl
from jax.experimental.pallas import tpu as pltpu
from jax.sharding import PartitionSpec as P

HEADS = 16
HDIM = 72
LANES = 128
HALF = 64
FOLD = 40
F32 = jnp.float32
BF16 = jnp.bfloat16
LIMIT = 56 * 1024 * 1024
SMALL = pl.CostEstimate(flops=1000, bytes_accessed=1000, transcendentals=0)
LARGE = pl.CostEstimate(flops=10**12, bytes_accessed=10**8, transcendentals=0)


def vmem_specs(count):
    return [pl.BlockSpec(memory_space=pltpu.VMEM)] * count


def low_lanes(rows):
    return lax.broadcasted_iota(jnp.int32, (rows, LANES), 1) < HALF


def swap(block):
    return pltpu.roll(block, HALF, 1)


def pack_kernel(q_ref, k_ref, v_ref, g_ref, out_ref):
    for frame in range(2):
        for pair, (first, second) in enumerate(((q_ref, k_ref), (v_ref, g_ref))):
            rows = jnp.concatenate([first[frame], second[frame]], axis=0).astype(F32)
            columns = rows.T
            for head in range(HEADS):
                out_ref[frame * HEADS + head, pair] = columns[
                    head * HDIM : (head + 1) * HDIM
                ].astype(BF16)


def pack(q, k, v, g):
    return pl.pallas_call(
        pack_kernel,
        out_shape=jax.ShapeDtypeStruct((2 * HEADS, 2, HDIM, LANES), BF16),
        in_specs=vmem_specs(4),
        out_specs=pl.BlockSpec(memory_space=pltpu.VMEM),
        compiler_params=pltpu.CompilerParams(vmem_limit_bytes=LIMIT),
        cost_estimate=SMALL,
        name="spatial_pack",
    )(q, k, v, g)


def attend_kernel(
    in_ref, out_ref, q_t, k_t, g_t, q_n, k_n, v_n, g_n, s_buf, p_buf, dq_t, dk_n, dv_n, *, step
):
    length = q_t.shape[1]
    pairs = length // LANES
    scale = 1.0 / math.sqrt(HDIM)
    power = scale * math.log2(math.e)

    def split(j, pair):
        first = in_ref[2 * j, pair].astype(F32)
        second = in_ref[2 * j + 1, pair].astype(F32)
        low = low_lanes(HDIM)
        return (
            jnp.where(low, first, swap(second)),
            jnp.where(low, swap(first), second),
        )

    for j in range(pairs):
        at = slice(j * LANES, (j + 1) * LANES)
        q, k = split(j, 0)
        v, g = split(j, 1)
        q_t[:, at] = q.astype(BF16)
        k_t[:, at] = k.astype(BF16)
        g_t[:, at] = g.astype(BF16)
        q_n[at, :] = q.T.astype(BF16)
        k_n[at, :] = k.T.astype(BF16)
        v_n[at, :] = v.T.astype(BF16)
        g_n[at, :] = g.T.astype(BF16)

    blocks = length // step

    def products(i, slot):
        at = pl.ds(pl.multiple_of(i * step, step), step)
        s_buf[slot] = jnp.dot(k_n[...], q_t[:, at], preferred_element_type=F32)
        p_buf[slot] = jnp.dot(v_n[...], g_t[:, at], preferred_element_type=F32)

    def rest(i, slot, first):
        at = pl.ds(pl.multiple_of(i * step, step), step)
        scores = s_buf[slot]
        peak = jnp.max(scores, axis=0, keepdims=True)
        raised = jnp.exp2((scores - peak) * power)
        over = 1.0 / jnp.sum(raised, axis=0, keepdims=True)
        grads = p_buf[slot]
        inner = jnp.sum(raised * grads, axis=0, keepdims=True) * over
        weights = raised * over
        low_w = weights.astype(BF16)
        low_s = (weights * (grads - inner)).astype(BF16)
        dv = jnp.dot(low_w, g_n[at, :], preferred_element_type=F32)
        dk = jnp.dot(low_s, q_n[at, :], preferred_element_type=F32)
        if first:
            dv_n[...] = dv
            dk_n[...] = dk
        else:
            dv_n[...] += dv
            dk_n[...] += dk
        dq_t[:, at] = jnp.dot(k_t[...], low_s, preferred_element_type=F32) * scale

    products(0, 0)
    products(1, 1)
    rest(0, 0, True)

    def body(i, _):
        slot = lax.rem(i, 2)
        products(i + 1, 1 - slot)
        rest(i, slot, False)
        return 0

    lax.fori_loop(1, blocks - 1, body, 0)
    rest(blocks - 1, (blocks - 1) % 2, False)

    for j in range(pairs):
        at = slice(j * LANES, (j + 1) * LANES)
        dq = dq_t[:, at]
        dk = (dk_n[at, :] * scale).T
        dv = dv_n[at, :].T
        low = low_lanes(HDIM)
        low_f = low_lanes(FOLD)
        upper, lower = dv[:FOLD], dv[HDIM - FOLD :]
        out_ref[2 * j] = jnp.concatenate(
            [jnp.where(low, dq, swap(dk)), jnp.where(low_f, upper, swap(lower))], axis=0
        ).astype(BF16)
        out_ref[2 * j + 1] = jnp.concatenate(
            [jnp.where(low, swap(dq), dk), jnp.where(low_f, swap(upper), lower)], axis=0
        ).astype(BF16)


def attend(received, step=256):
    sources = received.shape[0]
    length = sources * HALF
    wide = pltpu.VMEM((HDIM, length), BF16)
    tall = pltpu.VMEM((length, HDIM), BF16)
    return pl.pallas_call(
        functools.partial(attend_kernel, step=step),
        out_shape=jax.ShapeDtypeStruct((sources, HDIM + FOLD, LANES), BF16),
        in_specs=vmem_specs(1),
        out_specs=pl.BlockSpec(memory_space=pltpu.VMEM),
        scratch_shapes=[
            wide, wide, wide, tall, tall, tall, tall,
            pltpu.VMEM((2, length, step), F32),
            pltpu.VMEM((2, length, step), F32),
            pltpu.VMEM((HDIM, length), F32),
            pltpu.VMEM((length, HDIM), F32),
            pltpu.VMEM((length, HDIM), F32),
        ],
        compiler_params=pltpu.CompilerParams(vmem_limit_bytes=LIMIT),
        cost_estimate=pl.CostEstimate(
            flops=10 * length * length * 256, bytes_accessed=2200000, transcendentals=length * length
        ),
        name="spatial_attention",
    )(received)


def unpack_kernel(in_ref, dq_ref, dk_ref, dv_ref, dw_ref, full):
    low = low_lanes(HEADS * HDIM)
    values = []
    for frame in range(2):
        items = [
            in_ref[frame * HEADS + head, : HDIM + FOLD].astype(F32) for head in range(HEADS)
        ]
        both = jnp.concatenate([item[:HDIM] for item in items], axis=0).T.astype(BF16)
        dq_ref[frame] = both[:HALF]
        dk_ref[frame] = both[HALF:]
        values.append(
            jnp.concatenate(
                [
                    jnp.concatenate([item[HDIM:], swap(item[2 * FOLD :])], axis=0)
                    for item in items
                ],
                axis=0,
            )
        )
    both = jnp.where(low, values[0], swap(values[1])).T.astype(BF16)
    dv_ref[0] = both[:HALF]
    dv_ref[1] = both[HALF:]
    for s in range(2 * HEADS):
        half = 144 * (s % 2)
        unfold(
            in_ref[s].astype(F32)[HDIM + FOLD :], full, half + 8 * (s // 2), half + 128 + s // 2
        )
    dw_ref[...] = full[...].T[:288]


def unpack(received):
    shape = jax.ShapeDtypeStruct((2, HALF, HEADS * HDIM), BF16)
    return pl.pallas_call(
        unpack_kernel,
        out_shape=(shape, shape, shape, jax.ShapeDtypeStruct((288, 288), F32)),
        in_specs=vmem_specs(1),
        out_specs=tuple(vmem_specs(4)),
        scratch_shapes=[pltpu.VMEM((288, 3 * LANES), F32)],
        compiler_params=pltpu.CompilerParams(vmem_limit_bytes=LIMIT),
        name="spatial_unpack",
    )(received)


def flip(block):
    return pltpu.roll(block, HALF, 1)


def fold_tail(rest, r):
    return jnp.concatenate(
        [jnp.zeros((rest.shape[0], 32), F32), rest[:, 96 * r : 96 * r + 96]], axis=1
    )


def send_pack_kernel(me_ref, q_ref, k_ref, v_ref, out0, out1, out2, out3, held):
    for part, ref in enumerate((q_ref, k_ref, v_ref)):
        rows = jnp.concatenate([ref[0], ref[1]], axis=0).astype(F32)
        columns = rows.T.astype(BF16)
        at = slice(part * LANES, (part + 1) * LANES)
        held[0, :, at] = columns[:288]
        held[1, :, at] = columns[288:576]
        held[2, :, at] = columns[576:864]
        held[3, :, at] = columns[864:]
    me = me_ref[0]
    for shift, out in enumerate((out0, out1, out2, out3)):
        out[...] = held[lax.rem(me + shift, 4)]


def send_pack(me, q, k, v):
    shape = jax.ShapeDtypeStruct((288, 3 * LANES), BF16)
    return pl.pallas_call(
        send_pack_kernel,
        out_shape=(shape,) * 4,
        in_specs=[pl.BlockSpec(memory_space=pltpu.SMEM)] + vmem_specs(3),
        out_specs=tuple(vmem_specs(4)),
        scratch_shapes=[pltpu.VMEM((4, 288, 3 * LANES), BF16)],
        compiler_params=pltpu.CompilerParams(vmem_limit_bytes=LIMIT),
        cost_estimate=LARGE,
        name="temporal_pack",
    )(me, q, k, v)


def rows_of(values):
    return jnp.concatenate([jnp.sum(value, axis=0, keepdims=True) for value in values], axis=0)


def frame_weights(query, keys):
    scores = rows_of([query * key for key in keys])
    peak = jnp.max(scores, axis=0, keepdims=True)
    raised = jnp.exp2((scores - peak) * (math.log2(math.e) / math.sqrt(HDIM)))
    return raised / jnp.sum(raised, axis=0, keepdims=True)


def rounded(value):
    return value.astype(BF16).astype(F32)


def head_rows(wide, head, part):
    rows = pl.ds(pl.multiple_of(head * HDIM, 8), HDIM)
    at = slice(part * LANES, (part + 1) * LANES)
    return [wide[shift, rows, at] for shift in range(4)]


def both_ways(blocks):
    out = []
    for block in blocks:
        out += [block, flip(block)]
    return out


def tout_kernel(me_ref, in0, in1, in2, in3, out_ref, wide, total):
    for shift, ref in enumerate((in0, in1, in2, in3)):
        wide[shift] = ref[...].astype(F32)

    def body(head, _):
        queries = head_rows(wide, head, 0)
        keys = both_ways(head_rows(wide, head, 1))
        values = both_ways(head_rows(wide, head, 2))
        for shift in range(4):
            weights = rounded(frame_weights(queries[shift], keys))
            out = weights[0:1] * values[0]
            for j in range(1, 8):
                out = out + weights[j : j + 1] * values[j]
            total[shift, pl.ds(pl.multiple_of(head * HDIM, 8), HDIM)] = out
        return 0

    lax.fori_loop(0, 4, body, 0)
    me = me_ref[0]
    for shift in range(4):
        out_ref[lax.rem(me + 4 - shift, 4)] = total[shift].astype(BF16)


def temporal_out(me, pieces):
    return pl.pallas_call(
        tout_kernel,
        out_shape=jax.ShapeDtypeStruct((4, 288, LANES), BF16),
        in_specs=[pl.BlockSpec(memory_space=pltpu.SMEM)] + vmem_specs(4),
        out_specs=pl.BlockSpec(memory_space=pltpu.VMEM),
        scratch_shapes=[
            pltpu.VMEM((4, 288, 3 * LANES), F32),
            pltpu.VMEM((4, 288, LANES), F32),
        ],
        compiler_params=pltpu.CompilerParams(vmem_limit_bytes=LIMIT),
        cost_estimate=SMALL,
        name="temporal_tout",
    )(me, *pieces)


def partial_kernel(
    me_ref, tout_ref, grad_ref, w_ref, keep_ref, send_ref, slice_ref, full, stage, rows, *, scale
):
    total = jnp.dot(tout_ref[0], grad_ref[0], preferred_element_type=F32)
    for a in range(1, 4):
        total = total + jnp.dot(tout_ref[a], grad_ref[a], preferred_element_type=F32)
    total = total * scale
    full[0] = total[:144]
    full[1] = total[144:]
    core, eighth = me_ref[2], me_ref[1]
    keep_ref[...] = full[core]
    send_ref[...] = full[1 - core].astype(BF16)

    rows[...] = w_ref[...].astype(F32)
    stage[...] = jnp.zeros_like(stage)
    tail = rows[256:288]
    index = lax.broadcasted_iota(jnp.int32, tail.shape, 0)
    for k in range(4):
        at = slice(288 * k, 288 * (k + 1))
        stage[0:8, at] = rows[pl.ds(pl.multiple_of(32 * eighth + 8 * k, 8), 8)]
        stage[8:9, at] = jnp.sum(
            jnp.where(index == 4 * eighth + k, tail, 0.0), axis=0, keepdims=True
        )
    slice_ref[...] = stage[...].astype(BF16)


def weight_partial(me, tout, grads, w, scale):
    return pl.pallas_call(
        functools.partial(partial_kernel, scale=scale),
        out_shape=(
            jax.ShapeDtypeStruct((144, 1152), F32),
            jax.ShapeDtypeStruct((144, 1152), BF16),
            jax.ShapeDtypeStruct((16, 1152), BF16),
        ),
        in_specs=[pl.BlockSpec(memory_space=pltpu.SMEM)] + vmem_specs(3),
        out_specs=tuple(vmem_specs(3)),
        scratch_shapes=[
            pltpu.VMEM((2, 144, 1152), F32),
            pltpu.VMEM((16, 1152), F32),
            pltpu.VMEM((288, 288), F32),
        ],
        compiler_params=pltpu.CompilerParams(vmem_limit_bytes=LIMIT),
        cost_estimate=SMALL,
        name="weight_partial",
    )(me, tout, grads, w)


def weight_split_kernel(keep_ref, got_ref, out_ref, full, part):
    full[...] = keep_ref[...] + got_ref[...].astype(F32)
    part[...] = jnp.zeros_like(part)
    row = lax.broadcasted_iota(jnp.int32, (16, 8, LANES), 1)
    for d in range(4):
        part[:, :288] = full[:, d * 288 : (d + 1) * 288]
        tiles = [
            part[:128, tile * LANES : (tile + 1) * LANES].reshape(16, 8, LANES)
            for tile in range(3)
        ]
        rest = part[128:144, :]
        for r in range(3):
            tiles[2] = tiles[2] + jnp.where(row == r, fold_tail(rest, r)[:, None, :], 0.0)
        out_ref[d * 16 : (d + 1) * 16] = jnp.concatenate(tiles, axis=1).astype(BF16)


def fold_tail(rest, r):
    return jnp.concatenate(
        [jnp.zeros((rest.shape[0], 32), F32), rest[:, 96 * r : 96 * r + 96]], axis=1
    )


def weight_split(keep, got):
    return pl.pallas_call(
        weight_split_kernel,
        out_shape=jax.ShapeDtypeStruct((64, 24, LANES), BF16),
        in_specs=vmem_specs(2),
        out_specs=pl.BlockSpec(memory_space=pltpu.VMEM),
        scratch_shapes=[pltpu.VMEM((144, 1152), F32), pltpu.VMEM((144, 3 * LANES), F32)],
        compiler_params=pltpu.CompilerParams(vmem_limit_bytes=LIMIT),
        cost_estimate=SMALL,
        name="weight_split",
    )(keep, got)


def unfold(block, full, start, last):
    for tile in range(3):
        at = slice(tile * LANES, (tile + 1) * LANES)
        full[start : start + 8, at] = block[tile * 8 : tile * 8 + 8]
    for r in range(3):
        full[last : last + 1, 96 * r : 96 * r + 96] = block[16 + r : 17 + r, 32:]


def weight_join_kernel(spatial_ref, in_ref, out_ref):
    total = in_ref[0].astype(F32)
    for s in range(1, 64):
        total = total + in_ref[s].astype(F32)
    copy = total.astype(BF16)
    for s in range(32):
        out_ref[s, : HDIM + FOLD] = spatial_ref[s]
        out_ref[s, HDIM + FOLD :] = copy


def weight_join(spatial, received):
    return pl.pallas_call(
        weight_join_kernel,
        out_shape=jax.ShapeDtypeStruct((32, HDIM + FOLD + 24, LANES), BF16),
        in_specs=vmem_specs(2),
        out_specs=pl.BlockSpec(memory_space=pltpu.VMEM),
        compiler_params=pltpu.CompilerParams(vmem_limit_bytes=LIMIT),
        cost_estimate=SMALL,
        name="weight_join",
    )(spatial, received)


def temporal_kernel(
    me_ref, in0, in1, in2, in3, grad_ref, w_ref, out0, out1, out2, out3, wide, back, full
):
    me = me_ref[0]
    for d in range(4):
        for y in range(4):
            for c in range(2):
                block = w_ref[d * 8 + y * 2 + c].astype(F32)
                eighth = 4 * c + y
                for k in range(4):
                    at = slice(288 * k, 288 * (k + 1))
                    start = d * 288 + 32 * eighth + 8 * k
                    full[start : start + 8] = block[0:8, at]
                    start = d * 288 + 256 + 4 * eighth + k
                    full[start : start + 1] = block[8:9, at]
    w = full[...].astype(BF16)
    for shift, ref in enumerate((in0, in1, in2, in3)):
        wide[shift, :, : 3 * LANES] = ref[...].astype(F32)
        grads = grad_ref[lax.rem(me + 4 - shift, 4)]
        tgrad = rounded(jnp.dot(grads, w, preferred_element_type=F32))
        wide[shift, :, 3 * LANES :] = tgrad.T
    scale = 1.0 / math.sqrt(HDIM)

    def body(head, _):
        rows = pl.ds(pl.multiple_of(head * HDIM, 8), HDIM)
        queries = head_rows(wide, head, 0)
        keys = both_ways(head_rows(wide, head, 1))
        values = both_ways(head_rows(wide, head, 2))
        grads = head_rows(wide, head, 3)
        low_w, low_s = [], []
        for shift in range(4):
            weights = frame_weights(queries[shift], keys)
            pgrad = rows_of([grads[shift] * value for value in values])
            inner = jnp.sum(weights * pgrad, axis=0, keepdims=True)
            low_w.append(rounded(weights))
            low_s.append(rounded(weights * (pgrad - inner)))
            dq = low_s[shift][0:1] * keys[0]
            for j in range(1, 8):
                dq = dq + low_s[shift][j : j + 1] * keys[j]
            back[shift, rows, 0:LANES] = dq * scale
        for b in range(4):
            for part, (coefs, terms, factor) in enumerate(
                ((low_s, queries, scale), (low_w, grads, 1.0)), 1
            ):
                sums = []
                for way in range(2):
                    j = 2 * b + way
                    total = coefs[0][j : j + 1] * terms[0]
                    for shift in range(1, 4):
                        total = total + coefs[shift][j : j + 1] * terms[shift]
                    sums.append(total)
                back[b, rows, part * LANES : (part + 1) * LANES] = (
                    sums[0] + flip(sums[1])
                ) * factor
        return 0

    lax.fori_loop(0, 4, body, 0)
    for shift, out in enumerate((out0, out1, out2, out3)):
        out[...] = back[shift].astype(BF16)


def temporal_back(me, pieces, grads, w):
    shape = jax.ShapeDtypeStruct((288, 3 * LANES), BF16)
    return pl.pallas_call(
        temporal_kernel,
        out_shape=(shape,) * 4,
        in_specs=[pl.BlockSpec(memory_space=pltpu.SMEM)] + vmem_specs(6),
        out_specs=tuple(vmem_specs(4)),
        scratch_shapes=[
            pltpu.VMEM((4, 288, 4 * LANES), F32),
            pltpu.VMEM((4, 288, 3 * LANES), F32),
            pltpu.VMEM((1152, 288), F32),
        ],
        compiler_params=pltpu.CompilerParams(vmem_limit_bytes=LIMIT),
        cost_estimate=LARGE,
        name="temporal_back",
    )(me, *pieces, grads, w)


def receive_kernel(me_ref, in0, in1, in2, in3, dq_ref, dk_ref, dv_ref, held):
    me = me_ref[0]
    for shift, ref in enumerate((in0, in1, in2, in3)):
        held[lax.rem(me + shift, 4)] = ref[...]
    for part, out in enumerate((dq_ref, dk_ref, dv_ref)):
        at = slice(part * LANES, (part + 1) * LANES)
        columns = jnp.concatenate([held[t, :, at] for t in range(4)], axis=0).astype(F32)
        rows = columns.T.astype(BF16)
        out[0] = rows[:HALF]
        out[1] = rows[HALF:]


def receive(me, pieces):
    shape = jax.ShapeDtypeStruct((2, HALF, HEADS * HDIM), BF16)
    return pl.pallas_call(
        receive_kernel,
        out_shape=(shape,) * 3,
        in_specs=[pl.BlockSpec(memory_space=pltpu.SMEM)] + vmem_specs(4),
        out_specs=tuple(vmem_specs(3)),
        scratch_shapes=[pltpu.VMEM((4, 288, 3 * LANES), BF16)],
        compiler_params=pltpu.CompilerParams(vmem_limit_bytes=LIMIT),
        name="temporal_unpack",
    )(me, *pieces)


SWAP_CORE = [(0, 1), (1, 0)]
RING = [[(i, (i + s) % 4) for i in range(4)] for s in (1, 2, 3)]
RING_BACK = [[(i, (i - s) % 4) for i in range(4)] for s in (1, 2, 3)]


def shards(
    q_spatial,
    k_spatial,
    v_spatial,
    grad_spatial,
    q_temporal,
    k_temporal,
    v_temporal,
    grad_out,
    w_tout,
):
    core = lax.axis_index("c")
    me = jnp.stack([lax.axis_index("tm"), 4 * core + lax.axis_index("y"), core])
    space = ("z", "y", "c")
    grads = lax.all_gather(grad_out, "tm", axis=1, tiled=True).reshape(4, LANES, 1152)
    packed = pack(q_spatial[0], k_spatial[0], v_spatial[0], grad_spatial[0])
    packed, q, k, v = lax.optimization_barrier(
        (packed, q_temporal[0], k_temporal[0], v_temporal[0])
    )
    received = lax.all_to_all(packed, space, split_axis=0, concat_axis=0, tiled=True)

    sends = send_pack(me, q, k, v)
    pieces = (sends[0],) + tuple(
        lax.ppermute(sends[shift], "tm", RING[shift - 1]) for shift in (1, 2, 3)
    )
    tout = temporal_out(me, pieces)
    keep, send, eighth = weight_partial(me, tout, grads, w_tout, 1.0 / math.sqrt(65536))
    weight = lax.all_gather(eighth, ("dp", "y", "c"), axis=0, tiled=True).reshape(32, 16, 1152)
    blocks = weight_split(keep, lax.ppermute(send, "c", SWAP_CORE))

    received, blocks = lax.optimization_barrier((received, blocks))
    blocks = lax.all_to_all(blocks, ("dp", "z", "y"), split_axis=0, concat_axis=0, tiled=True)
    results = weight_join(attend(received), blocks)
    results, *pieces = lax.optimization_barrier((results,) + pieces)
    returned = lax.all_to_all(results, space, split_axis=0, concat_axis=0, tiled=True)

    backs = temporal_back(me, pieces, grads, weight)
    homes = (backs[0],) + tuple(
        lax.ppermute(backs[shift], "tm", RING_BACK[shift - 1]) for shift in (1, 2, 3)
    )
    dq_t, dk_t, dv_t = receive(me, homes)
    dq, dk, dv, weight_grad = unpack(returned)
    return (dq[None], dk[None], dv[None], dq_t[None], dk_t[None], dv_t[None], weight_grad)


def solution(mesh):
    sizes = (mesh.shape["dp"], mesh.shape["tm"], 4, 4, 2)
    split = jax.sharding.Mesh(mesh.devices.reshape(sizes), ("dp", "tm", "z", "y", "c"))
    field = P("dp", "tm", ("z", "y", "c"), None)
    return jax.shard_map(
        shards,
        mesh=split,
        in_specs=(field,) * 8 + (P("dp", "tm"),),
        out_specs=(field,) * 6 + (P("dp", "tm"),),
        check_vma=False,
    )
```

```python
import math
import functools
import jax
import jax.numpy as jnp
from jax import lax
from jax.experimental import pallas as pl
from jax.experimental.pallas import tpu as pltpu
from jax.sharding import PartitionSpec as P

HEADS = 16
HDIM = 72
LANES = 128
HALF = 64
FOLD = 40
F32 = jnp.float32
BF16 = jnp.bfloat16
LIMIT = 56 * 1024 * 1024
SMALL = pl.CostEstimate(flops=1000, bytes_accessed=1000, transcendentals=0)
LARGE = pl.CostEstimate(flops=10**12, bytes_accessed=10**8, transcendentals=0)


def vmem_specs(count):
    return [pl.BlockSpec(memory_space=pltpu.VMEM)] * count


def low_lanes(rows):
    return lax.broadcasted_iota(jnp.int32, (rows, LANES), 1) < HALF


def swap(block):
    return pltpu.roll(block, HALF, 1)


def pack_kernel(me_ref, q_ref, k_ref, v_ref, g_ref, w_ref, out_ref, slice_ref, stage, rows):
    for frame in range(2):
        for pair, (first, second) in enumerate(((q_ref, k_ref), (v_ref, g_ref))):
            both = jnp.concatenate([first[frame], second[frame]], axis=0).astype(F32)
            columns = both.T
            for head in range(HEADS):
                out_ref[frame * HEADS + head, pair] = columns[
                    head * HDIM : (head + 1) * HDIM
                ].astype(BF16)

    eighth = me_ref[1]
    rows[...] = w_ref[...].astype(F32)
    stage[...] = jnp.zeros_like(stage)
    tail = rows[256:288]
    index = lax.broadcasted_iota(jnp.int32, tail.shape, 0)
    for k in range(4):
        at = slice(288 * k, 288 * (k + 1))
        stage[0:8, at] = rows[pl.ds(pl.multiple_of(32 * eighth + 8 * k, 8), 8)]
        stage[8:9, at] = jnp.sum(
            jnp.where(index == 4 * eighth + k, tail, 0.0), axis=0, keepdims=True
        )
    slice_ref[...] = stage[...].astype(BF16)


def pack(me, q, k, v, g, w):
    return pl.pallas_call(
        pack_kernel,
        out_shape=(
            jax.ShapeDtypeStruct((2 * HEADS, 2, HDIM, LANES), BF16),
            jax.ShapeDtypeStruct((16, 1152), BF16),
        ),
        in_specs=[pl.BlockSpec(memory_space=pltpu.SMEM)] + vmem_specs(5),
        out_specs=tuple(vmem_specs(2)),
        scratch_shapes=[pltpu.VMEM((16, 1152), F32), pltpu.VMEM((288, 288), F32)],
        compiler_params=pltpu.CompilerParams(vmem_limit_bytes=LIMIT),
        cost_estimate=SMALL,
        name="spatial_pack",
    )(me, q, k, v, g, w)


def attend_kernel(
    in_ref, out_ref, q_t, k_t, g_t, q_n, k_n, v_n, g_n, s_buf, p_buf, dq_t, dk_n, dv_n, *, step
):
    length = q_t.shape[1]
    pairs = length // LANES
    scale = 1.0 / math.sqrt(HDIM)
    power = scale * math.log2(math.e)

    def split(j, pair):
        first = in_ref[2 * j, pair].astype(F32)
        second = in_ref[2 * j + 1, pair].astype(F32)
        low = low_lanes(HDIM)
        return (
            jnp.where(low, first, swap(second)),
            jnp.where(low, swap(first), second),
        )

    for j in range(pairs):
        at = slice(j * LANES, (j + 1) * LANES)
        q, k = split(j, 0)
        v, g = split(j, 1)
        q_t[:, at] = q.astype(BF16)
        k_t[:, at] = k.astype(BF16)
        g_t[:, at] = g.astype(BF16)
        q_n[at, :] = q.T.astype(BF16)
        k_n[at, :] = k.T.astype(BF16)
        v_n[at, :] = v.T.astype(BF16)
        g_n[at, :] = g.T.astype(BF16)

    blocks = length // step

    def products(i, slot):
        at = pl.ds(pl.multiple_of(i * step, step), step)
        s_buf[slot] = jnp.dot(k_n[...], q_t[:, at], preferred_element_type=F32)
        p_buf[slot] = jnp.dot(v_n[...], g_t[:, at], preferred_element_type=F32)

    def rest(i, slot, first):
        at = pl.ds(pl.multiple_of(i * step, step), step)
        scores = s_buf[slot]
        peak = jnp.max(scores, axis=0, keepdims=True)
        raised = jnp.exp2((scores - peak) * power)
        over = 1.0 / jnp.sum(raised, axis=0, keepdims=True)
        grads = p_buf[slot]
        inner = jnp.sum(raised * grads, axis=0, keepdims=True) * over
        weights = raised * over
        low_w = weights.astype(BF16)
        low_s = (weights * (grads - inner)).astype(BF16)
        dv = jnp.dot(low_w, g_n[at, :], preferred_element_type=F32)
        dk = jnp.dot(low_s, q_n[at, :], preferred_element_type=F32)
        if first:
            dv_n[...] = dv
            dk_n[...] = dk
        else:
            dv_n[...] += dv
            dk_n[...] += dk
        dq_t[:, at] = jnp.dot(k_t[...], low_s, preferred_element_type=F32) * scale

    products(0, 0)
    products(1, 1)
    rest(0, 0, True)

    def body(i, _):
        slot = lax.rem(i, 2)
        products(i + 1, 1 - slot)
        rest(i, slot, False)
        return 0

    lax.fori_loop(1, blocks - 1, body, 0)
    rest(blocks - 1, (blocks - 1) % 2, False)

    for j in range(pairs):
        at = slice(j * LANES, (j + 1) * LANES)
        dq = dq_t[:, at]
        dk = (dk_n[at, :] * scale).T
        dv = dv_n[at, :].T
        low = low_lanes(HDIM)
        low_f = low_lanes(FOLD)
        upper, lower = dv[:FOLD], dv[HDIM - FOLD :]
        out_ref[2 * j] = jnp.concatenate(
            [jnp.where(low, dq, swap(dk)), jnp.where(low_f, upper, swap(lower))], axis=0
        ).astype(BF16)
        out_ref[2 * j + 1] = jnp.concatenate(
            [jnp.where(low, swap(dq), dk), jnp.where(low_f, swap(upper), lower)], axis=0
        ).astype(BF16)


def attend(received, step=256):
    sources = received.shape[0]
    length = sources * HALF
    wide = pltpu.VMEM((HDIM, length), BF16)
    tall = pltpu.VMEM((length, HDIM), BF16)
    return pl.pallas_call(
        functools.partial(attend_kernel, step=step),
        out_shape=jax.ShapeDtypeStruct((sources, HDIM + FOLD, LANES), BF16),
        in_specs=vmem_specs(1),
        out_specs=pl.BlockSpec(memory_space=pltpu.VMEM),
        scratch_shapes=[
            wide, wide, wide, tall, tall, tall, tall,
            pltpu.VMEM((2, length, step), F32),
            pltpu.VMEM((2, length, step), F32),
            pltpu.VMEM((HDIM, length), F32),
            pltpu.VMEM((length, HDIM), F32),
            pltpu.VMEM((length, HDIM), F32),
        ],
        compiler_params=pltpu.CompilerParams(vmem_limit_bytes=LIMIT),
        cost_estimate=pl.CostEstimate(
            flops=10 * length * length * 256, bytes_accessed=2200000, transcendentals=length * length
        ),
        name="spatial_attention",
    )(received)


def unpack_kernel(in_ref, dq_ref, dk_ref, dv_ref, dw_ref, full):
    low = low_lanes(HEADS * HDIM)
    values = []
    for frame in range(2):
        items = [
            in_ref[frame * HEADS + head, : HDIM + FOLD].astype(F32) for head in range(HEADS)
        ]
        both = jnp.concatenate([item[:HDIM] for item in items], axis=0).T.astype(BF16)
        dq_ref[frame] = both[:HALF]
        dk_ref[frame] = both[HALF:]
        values.append(
            jnp.concatenate(
                [
                    jnp.concatenate([item[HDIM:], swap(item[2 * FOLD :])], axis=0)
                    for item in items
                ],
                axis=0,
            )
        )
    both = jnp.where(low, values[0], swap(values[1])).T.astype(BF16)
    dv_ref[0] = both[:HALF]
    dv_ref[1] = both[HALF:]
    for s in range(2 * HEADS):
        half = 144 * (s % 2)
        unfold(
            in_ref[s].astype(F32)[HDIM + FOLD :], full, half + 8 * (s // 2), half + 128 + s // 2
        )
    dw_ref[...] = full[...].T[:288]


def unpack(received):
    shape = jax.ShapeDtypeStruct((2, HALF, HEADS * HDIM), BF16)
    return pl.pallas_call(
        unpack_kernel,
        out_shape=(shape, shape, shape, jax.ShapeDtypeStruct((288, 288), F32)),
        in_specs=vmem_specs(1),
        out_specs=tuple(vmem_specs(4)),
        scratch_shapes=[pltpu.VMEM((288, 3 * LANES), F32)],
        compiler_params=pltpu.CompilerParams(vmem_limit_bytes=LIMIT),
        name="spatial_unpack",
    )(received)


def flip(block):
    return pltpu.roll(block, HALF, 1)


def fold_tail(rest, r):
    return jnp.concatenate(
        [jnp.zeros((rest.shape[0], 32), F32), rest[:, 96 * r : 96 * r + 96]], axis=1
    )


def send_pack_kernel(me_ref, q_ref, k_ref, v_ref, g_ref, out0, out1, out2, out3, held):
    for part, ref in enumerate((q_ref, k_ref, v_ref)):
        rows = jnp.concatenate([ref[0], ref[1]], axis=0).astype(F32)
        columns = rows.T.astype(BF16)
        at = slice(part * LANES, (part + 1) * LANES)
        held[0, :, at] = columns[:288]
        held[1, :, at] = columns[288:576]
        held[2, :, at] = columns[576:864]
        held[3, :, at] = columns[864:]
    me = me_ref[0]
    grads = jnp.concatenate([g_ref[0], g_ref[1]], axis=0)
    for shift, out in enumerate((out0, out1, out2, out3)):
        out[:288] = held[lax.rem(me + shift, 4)]
        for third in range(3):
            out[288 + LANES * third : 288 + LANES * (third + 1)] = grads[
                :, 384 * third : 384 * (third + 1)
            ]


def send_pack(me, q, k, v, g):
    shape = jax.ShapeDtypeStruct((672, 3 * LANES), BF16)
    return pl.pallas_call(
        send_pack_kernel,
        out_shape=(shape,) * 4,
        in_specs=[pl.BlockSpec(memory_space=pltpu.SMEM)] + vmem_specs(4),
        out_specs=tuple(vmem_specs(4)),
        scratch_shapes=[pltpu.VMEM((4, 288, 3 * LANES), BF16)],
        compiler_params=pltpu.CompilerParams(vmem_limit_bytes=LIMIT),
        cost_estimate=LARGE,
        name="temporal_pack",
    )(me, q, k, v, g)


def piece_grads(ref):
    return jnp.concatenate(
        [ref[288 + LANES * third : 288 + LANES * (third + 1)] for third in range(3)], axis=1
    )


def rows_of(values):
    return jnp.concatenate([jnp.sum(value, axis=0, keepdims=True) for value in values], axis=0)


def frame_weights(query, keys):
    scores = rows_of([query * key for key in keys])
    peak = jnp.max(scores, axis=0, keepdims=True)
    raised = jnp.exp2((scores - peak) * (math.log2(math.e) / math.sqrt(HDIM)))
    return raised / jnp.sum(raised, axis=0, keepdims=True)


def rounded(value):
    return value.astype(BF16).astype(F32)


def head_rows(wide, head, part):
    rows = pl.ds(pl.multiple_of(head * HDIM, 8), HDIM)
    at = slice(part * LANES, (part + 1) * LANES)
    return [wide[shift, rows, at] for shift in range(4)]


def both_ways(blocks):
    out = []
    for block in blocks:
        out += [block, flip(block)]
    return out


def partial_kernel(me_ref, in0, in1, in2, in3, keep_ref, send_ref, wide, tout, full, *, scale):
    for shift, ref in enumerate((in0, in1, in2, in3)):
        wide[shift] = ref[:288].astype(F32)

    def body(head, _):
        queries = head_rows(wide, head, 0)
        keys = both_ways(head_rows(wide, head, 1))
        values = both_ways(head_rows(wide, head, 2))
        for shift in range(4):
            weights = rounded(frame_weights(queries[shift], keys))
            out = weights[0:1] * values[0]
            for j in range(1, 8):
                out = out + weights[j : j + 1] * values[j]
            tout[shift, pl.ds(pl.multiple_of(head * HDIM, 8), HDIM)] = out
        return 0

    lax.fori_loop(0, 4, body, 0)
    total = None
    for shift, ref in enumerate((in0, in1, in2, in3)):
        term = jnp.dot(tout[shift].astype(BF16), piece_grads(ref), preferred_element_type=F32)
        total = term if total is None else total + term
    total = total * scale
    full[0] = total[:144]
    full[1] = total[144:]
    core = me_ref[2]
    keep_ref[...] = full[core]
    send_ref[...] = full[1 - core].astype(BF16)


def weight_partial(me, pieces, scale):
    return pl.pallas_call(
        functools.partial(partial_kernel, scale=scale),
        out_shape=(
            jax.ShapeDtypeStruct((144, 1152), F32),
            jax.ShapeDtypeStruct((144, 1152), BF16),
        ),
        in_specs=[pl.BlockSpec(memory_space=pltpu.SMEM)] + vmem_specs(4),
        out_specs=tuple(vmem_specs(2)),
        scratch_shapes=[
            pltpu.VMEM((4, 288, 3 * LANES), F32),
            pltpu.VMEM((4, 288, LANES), F32),
            pltpu.VMEM((2, 144, 1152), F32),
        ],
        compiler_params=pltpu.CompilerParams(vmem_limit_bytes=LIMIT),
        cost_estimate=SMALL,
        name="weight_partial",
    )(me, *pieces)


def weight_split_kernel(keep_ref, got_ref, out_ref, full, part):
    full[...] = keep_ref[...] + got_ref[...].astype(F32)
    part[...] = jnp.zeros_like(part)
    row = lax.broadcasted_iota(jnp.int32, (16, 8, LANES), 1)
    for d in range(4):
        part[:, :288] = full[:, d * 288 : (d + 1) * 288]
        tiles = [
            part[:128, tile * LANES : (tile + 1) * LANES].reshape(16, 8, LANES)
            for tile in range(3)
        ]
        rest = part[128:144, :]
        for r in range(3):
            tiles[2] = tiles[2] + jnp.where(row == r, fold_tail(rest, r)[:, None, :], 0.0)
        out_ref[d * 16 : (d + 1) * 16] = jnp.concatenate(tiles, axis=1).astype(BF16)


def fold_tail(rest, r):
    return jnp.concatenate(
        [jnp.zeros((rest.shape[0], 32), F32), rest[:, 96 * r : 96 * r + 96]], axis=1
    )


def weight_split(keep, got):
    return pl.pallas_call(
        weight_split_kernel,
        out_shape=jax.ShapeDtypeStruct((64, 24, LANES), BF16),
        in_specs=vmem_specs(2),
        out_specs=pl.BlockSpec(memory_space=pltpu.VMEM),
        scratch_shapes=[pltpu.VMEM((144, 1152), F32), pltpu.VMEM((144, 3 * LANES), F32)],
        compiler_params=pltpu.CompilerParams(vmem_limit_bytes=LIMIT),
        cost_estimate=SMALL,
        name="weight_split",
    )(keep, got)


def unfold(block, full, start, last):
    for tile in range(3):
        at = slice(tile * LANES, (tile + 1) * LANES)
        full[start : start + 8, at] = block[tile * 8 : tile * 8 + 8]
    for r in range(3):
        full[last : last + 1, 96 * r : 96 * r + 96] = block[16 + r : 17 + r, 32:]


def weight_join_kernel(spatial_ref, in_ref, out_ref):
    total = in_ref[0].astype(F32)
    for s in range(1, 64):
        total = total + in_ref[s].astype(F32)
    copy = total.astype(BF16)
    for s in range(32):
        out_ref[s, : HDIM + FOLD] = spatial_ref[s]
        out_ref[s, HDIM + FOLD :] = copy


def weight_join(spatial, received):
    return pl.pallas_call(
        weight_join_kernel,
        out_shape=jax.ShapeDtypeStruct((32, HDIM + FOLD + 24, LANES), BF16),
        in_specs=vmem_specs(2),
        out_specs=pl.BlockSpec(memory_space=pltpu.VMEM),
        compiler_params=pltpu.CompilerParams(vmem_limit_bytes=LIMIT),
        cost_estimate=SMALL,
        name="weight_join",
    )(spatial, received)


def temporal_kernel(
    in0, in1, in2, in3, w_ref, out0, out1, out2, out3, wide, back, full
):
    for d in range(4):
        for y in range(4):
            for c in range(2):
                block = w_ref[d * 8 + y * 2 + c].astype(F32)
                eighth = 4 * c + y
                for k in range(4):
                    at = slice(288 * k, 288 * (k + 1))
                    start = d * 288 + 32 * eighth + 8 * k
                    full[start : start + 8] = block[0:8, at]
                    start = d * 288 + 256 + 4 * eighth + k
                    full[start : start + 1] = block[8:9, at]
    w = full[...].astype(BF16)
    for shift, ref in enumerate((in0, in1, in2, in3)):
        wide[shift, :, : 3 * LANES] = ref[:288].astype(F32)
        tgrad = rounded(jnp.dot(piece_grads(ref), w, preferred_element_type=F32))
        wide[shift, :, 3 * LANES :] = tgrad.T
    scale = 1.0 / math.sqrt(HDIM)

    def body(head, _):
        rows = pl.ds(pl.multiple_of(head * HDIM, 8), HDIM)
        queries = head_rows(wide, head, 0)
        keys = both_ways(head_rows(wide, head, 1))
        values = both_ways(head_rows(wide, head, 2))
        grads = head_rows(wide, head, 3)
        low_w, low_s = [], []
        for shift in range(4):
            weights = frame_weights(queries[shift], keys)
            pgrad = rows_of([grads[shift] * value for value in values])
            inner = jnp.sum(weights * pgrad, axis=0, keepdims=True)
            low_w.append(rounded(weights))
            low_s.append(rounded(weights * (pgrad - inner)))
            dq = low_s[shift][0:1] * keys[0]
            for j in range(1, 8):
                dq = dq + low_s[shift][j : j + 1] * keys[j]
            back[shift, rows, 0:LANES] = dq * scale
        for b in range(4):
            for part, (coefs, terms, factor) in enumerate(
                ((low_s, queries, scale), (low_w, grads, 1.0)), 1
            ):
                sums = []
                for way in range(2):
                    j = 2 * b + way
                    total = coefs[0][j : j + 1] * terms[0]
                    for shift in range(1, 4):
                        total = total + coefs[shift][j : j + 1] * terms[shift]
                    sums.append(total)
                back[b, rows, part * LANES : (part + 1) * LANES] = (
                    sums[0] + flip(sums[1])
                ) * factor
        return 0

    lax.fori_loop(0, 4, body, 0)
    for shift, out in enumerate((out0, out1, out2, out3)):
        out[...] = back[shift].astype(BF16)


def temporal_back(pieces, w):
    shape = jax.ShapeDtypeStruct((288, 3 * LANES), BF16)
    return pl.pallas_call(
        temporal_kernel,
        out_shape=(shape,) * 4,
        in_specs=vmem_specs(5),
        out_specs=tuple(vmem_specs(4)),
        scratch_shapes=[
            pltpu.VMEM((4, 288, 4 * LANES), F32),
            pltpu.VMEM((4, 288, 3 * LANES), F32),
            pltpu.VMEM((1152, 288), F32),
        ],
        compiler_params=pltpu.CompilerParams(vmem_limit_bytes=LIMIT),
        cost_estimate=LARGE,
        name="temporal_back",
    )(*pieces, w)


def receive_kernel(me_ref, in0, in1, in2, in3, dq_ref, dk_ref, dv_ref, held):
    me = me_ref[0]
    for shift, ref in enumerate((in0, in1, in2, in3)):
        held[lax.rem(me + shift, 4)] = ref[...]
    for part, out in enumerate((dq_ref, dk_ref, dv_ref)):
        at = slice(part * LANES, (part + 1) * LANES)
        columns = jnp.concatenate([held[t, :, at] for t in range(4)], axis=0).astype(F32)
        rows = columns.T.astype(BF16)
        out[0] = rows[:HALF]
        out[1] = rows[HALF:]


def receive(me, pieces):
    shape = jax.ShapeDtypeStruct((2, HALF, HEADS * HDIM), BF16)
    return pl.pallas_call(
        receive_kernel,
        out_shape=(shape,) * 3,
        in_specs=[pl.BlockSpec(memory_space=pltpu.SMEM)] + vmem_specs(4),
        out_specs=tuple(vmem_specs(3)),
        scratch_shapes=[pltpu.VMEM((4, 288, 3 * LANES), BF16)],
        compiler_params=pltpu.CompilerParams(vmem_limit_bytes=LIMIT),
        name="temporal_unpack",
    )(me, *pieces)


SWAP_CORE = [(0, 1), (1, 0)]
RING = [[(i, (i + s) % 4) for i in range(4)] for s in (1, 2, 3)]
RING_BACK = [[(i, (i - s) % 4) for i in range(4)] for s in (1, 2, 3)]


def shards(
    q_spatial,
    k_spatial,
    v_spatial,
    grad_spatial,
    q_temporal,
    k_temporal,
    v_temporal,
    grad_out,
    w_tout,
):
    core = lax.axis_index("c")
    me = jnp.stack([lax.axis_index("tm"), 4 * core + lax.axis_index("y"), core])
    space = ("z", "y", "c")
    packed, eighth = pack(
        me, q_spatial[0], k_spatial[0], v_spatial[0], grad_spatial[0], w_tout
    )
    weight = lax.all_gather(eighth, ("dp", "y", "c"), axis=0, tiled=True).reshape(32, 16, 1152)
    packed, q, k, v, g = lax.optimization_barrier(
        (packed, q_temporal[0], k_temporal[0], v_temporal[0], grad_out[0])
    )
    received = lax.all_to_all(packed, space, split_axis=0, concat_axis=0, tiled=True)

    sends = send_pack(me, q, k, v, g)
    pieces = (sends[0],) + tuple(
        lax.ppermute(sends[shift], "tm", RING[shift - 1]) for shift in (1, 2, 3)
    )
    keep, send = weight_partial(me, pieces, 1.0 / math.sqrt(65536))
    blocks = weight_split(keep, lax.ppermute(send, "c", SWAP_CORE))

    received, blocks = lax.optimization_barrier((received, blocks))
    blocks = lax.all_to_all(blocks, ("dp", "z", "y"), split_axis=0, concat_axis=0, tiled=True)
    results = weight_join(attend(received), blocks)
    results, *pieces = lax.optimization_barrier((results,) + pieces)
    returned = lax.all_to_all(results, space, split_axis=0, concat_axis=0, tiled=True)

    backs = temporal_back(pieces, weight)
    homes = (backs[0],) + tuple(
        lax.ppermute(backs[shift], "tm", RING_BACK[shift - 1]) for shift in (1, 2, 3)
    )
    dq_t, dk_t, dv_t = receive(me, homes)
    dq, dk, dv, weight_grad = unpack(returned)
    return (dq[None], dk[None], dv[None], dq_t[None], dk_t[None], dv_t[None], weight_grad)


def solution(mesh):
    sizes = (mesh.shape["dp"], mesh.shape["tm"], 4, 4, 2)
    split = jax.sharding.Mesh(mesh.devices.reshape(sizes), ("dp", "tm", "z", "y", "c"))
    field = P("dp", "tm", ("z", "y", "c"), None)
    return jax.shard_map(
        shards,
        mesh=split,
        in_specs=(field,) * 8 + (P("dp", "tm"),),
        out_specs=(field,) * 6 + (P("dp", "tm"),),
        check_vma=False,
    )
```

```python
import math
import functools
import jax
import jax.numpy as jnp
from jax import lax
from jax.experimental import pallas as pl
from jax.experimental.pallas import tpu as pltpu
from jax.sharding import PartitionSpec as P

HEADS = 16
HDIM = 72
LANES = 128
HALF = 64
CUTS = ((0, 40), (40, 80), (80, 112), (112, 144))
FOLD = 40
F32 = jnp.float32
BF16 = jnp.bfloat16
LIMIT = 56 * 1024 * 1024
SMALL = pl.CostEstimate(flops=1000, bytes_accessed=1000, transcendentals=0)
LARGE = pl.CostEstimate(flops=10**12, bytes_accessed=10**8, transcendentals=0)


def vmem_specs(count):
    return [pl.BlockSpec(memory_space=pltpu.VMEM)] * count


def low_lanes(rows):
    return lax.broadcasted_iota(jnp.int32, (rows, LANES), 1) < HALF


def swap(block):
    return pltpu.roll(block, HALF, 1)


def pack_kernel(me_ref, q_ref, k_ref, v_ref, g_ref, w_ref, out_ref, half_ref, stage, rows):
    for frame in range(2):
        for pair, (first, second) in enumerate(((q_ref, k_ref), (v_ref, g_ref))):
            both = jnp.concatenate([first[frame], second[frame]], axis=0).astype(F32)
            columns = both.T
            for head in range(HEADS):
                out_ref[frame * HEADS + head, pair] = columns[
                    head * HDIM : (head + 1) * HDIM
                ].astype(BF16)

    w = w_ref[...].astype(F32)
    rows[0] = w[:144]
    rows[1] = w[144:]
    half = rows[me_ref[2]]
    stage[...] = jnp.zeros_like(stage)
    for k, (start, end) in enumerate(CUTS):
        stage[: end - start, 288 * k : 288 * (k + 1)] = half[start:end]
    half_ref[...] = stage[...].astype(BF16)


def pack(me, q, k, v, g, w):
    return pl.pallas_call(
        pack_kernel,
        out_shape=(
            jax.ShapeDtypeStruct((2 * HEADS, 2, HDIM, LANES), BF16),
            jax.ShapeDtypeStruct((64, 1152), BF16),
        ),
        in_specs=[pl.BlockSpec(memory_space=pltpu.SMEM)] + vmem_specs(5),
        out_specs=tuple(vmem_specs(2)),
        scratch_shapes=[pltpu.VMEM((64, 1152), F32), pltpu.VMEM((2, 144, 288), F32)],
        compiler_params=pltpu.CompilerParams(vmem_limit_bytes=LIMIT),
        cost_estimate=SMALL,
        name="spatial_pack",
    )(me, q, k, v, g, w)


def attend_kernel(
    in_ref, out_ref, q_t, k_t, g_t, q_n, k_n, v_n, g_n, s_buf, p_buf, dq_t, dk_n, dv_n, *, step
):
    length = q_t.shape[1]
    pairs = length // LANES
    scale = 1.0 / math.sqrt(HDIM)
    power = scale * math.log2(math.e)

    def split(j, pair):
        first = in_ref[2 * j, pair].astype(F32)
        second = in_ref[2 * j + 1, pair].astype(F32)
        low = low_lanes(HDIM)
        return (
            jnp.where(low, first, swap(second)),
            jnp.where(low, swap(first), second),
        )

    for j in range(pairs):
        at = slice(j * LANES, (j + 1) * LANES)
        q, k = split(j, 0)
        v, g = split(j, 1)
        q_t[:, at] = q.astype(BF16)
        k_t[:, at] = k.astype(BF16)
        g_t[:, at] = g.astype(BF16)
        q_n[at, :] = q.T.astype(BF16)
        k_n[at, :] = k.T.astype(BF16)
        v_n[at, :] = v.T.astype(BF16)
        g_n[at, :] = g.T.astype(BF16)

    blocks = length // step

    def products(i, slot):
        at = pl.ds(pl.multiple_of(i * step, step), step)
        s_buf[slot] = jnp.dot(k_n[...], q_t[:, at], preferred_element_type=F32)
        p_buf[slot] = jnp.dot(v_n[...], g_t[:, at], preferred_element_type=F32)

    def rest(i, slot, first):
        at = pl.ds(pl.multiple_of(i * step, step), step)
        scores = s_buf[slot]
        peak = jnp.max(scores, axis=0, keepdims=True)
        raised = jnp.exp2((scores - peak) * power)
        over = 1.0 / jnp.sum(raised, axis=0, keepdims=True)
        grads = p_buf[slot]
        inner = jnp.sum(raised * grads, axis=0, keepdims=True) * over
        weights = raised * over
        low_w = weights.astype(BF16)
        low_s = (weights * (grads - inner)).astype(BF16)
        dv = jnp.dot(low_w, g_n[at, :], preferred_element_type=F32)
        dk = jnp.dot(low_s, q_n[at, :], preferred_element_type=F32)
        if first:
            dv_n[...] = dv
            dk_n[...] = dk
        else:
            dv_n[...] += dv
            dk_n[...] += dk
        dq_t[:, at] = jnp.dot(k_t[...], low_s, preferred_element_type=F32) * scale

    products(0, 0)
    products(1, 1)
    rest(0, 0, True)

    def body(i, _):
        slot = lax.rem(i, 2)
        products(i + 1, 1 - slot)
        rest(i, slot, False)
        return 0

    lax.fori_loop(1, blocks - 1, body, 0)
    rest(blocks - 1, (blocks - 1) % 2, False)

    for j in range(pairs):
        at = slice(j * LANES, (j + 1) * LANES)
        dq = dq_t[:, at]
        dk = (dk_n[at, :] * scale).T
        dv = dv_n[at, :].T
        low = low_lanes(HDIM)
        low_f = low_lanes(FOLD)
        upper, lower = dv[:FOLD], dv[HDIM - FOLD :]
        out_ref[2 * j] = jnp.concatenate(
            [jnp.where(low, dq, swap(dk)), jnp.where(low_f, upper, swap(lower))], axis=0
        ).astype(BF16)
        out_ref[2 * j + 1] = jnp.concatenate(
            [jnp.where(low, swap(dq), dk), jnp.where(low_f, swap(upper), lower)], axis=0
        ).astype(BF16)


def attend(received, step=256):
    sources = received.shape[0]
    length = sources * HALF
    wide = pltpu.VMEM((HDIM, length), BF16)
    tall = pltpu.VMEM((length, HDIM), BF16)
    return pl.pallas_call(
        functools.partial(attend_kernel, step=step),
        out_shape=jax.ShapeDtypeStruct((sources, HDIM + FOLD, LANES), BF16),
        in_specs=vmem_specs(1),
        out_specs=pl.BlockSpec(memory_space=pltpu.VMEM),
        scratch_shapes=[
            wide, wide, wide, tall, tall, tall, tall,
            pltpu.VMEM((2, length, step), F32),
            pltpu.VMEM((2, length, step), F32),
            pltpu.VMEM((HDIM, length), F32),
            pltpu.VMEM((length, HDIM), F32),
            pltpu.VMEM((length, HDIM), F32),
        ],
        compiler_params=pltpu.CompilerParams(vmem_limit_bytes=LIMIT),
        cost_estimate=pl.CostEstimate(
            flops=10 * length * length * 256, bytes_accessed=2200000, transcendentals=length * length
        ),
        name="spatial_attention",
    )(received)


def unpack_kernel(in_ref, dq_ref, dk_ref, dv_ref, dw_ref, full):
    low = low_lanes(HEADS * HDIM)
    values = []
    for frame in range(2):
        items = [
            in_ref[frame * HEADS + head, : HDIM + FOLD].astype(F32) for head in range(HEADS)
        ]
        both = jnp.concatenate([item[:HDIM] for item in items], axis=0).T.astype(BF16)
        dq_ref[frame] = both[:HALF]
        dk_ref[frame] = both[HALF:]
        values.append(
            jnp.concatenate(
                [
                    jnp.concatenate([item[HDIM:], swap(item[2 * FOLD :])], axis=0)
                    for item in items
                ],
                axis=0,
            )
        )
    both = jnp.where(low, values[0], swap(values[1])).T.astype(BF16)
    dv_ref[0] = both[:HALF]
    dv_ref[1] = both[HALF:]
    for s in range(2 * HEADS):
        half = 144 * (s % 2)
        unfold(
            in_ref[s].astype(F32)[HDIM + FOLD :], full, half + 8 * (s // 2), half + 128 + s // 2
        )
    dw_ref[...] = full[...].T[:288]


def unpack(received):
    shape = jax.ShapeDtypeStruct((2, HALF, HEADS * HDIM), BF16)
    return pl.pallas_call(
        unpack_kernel,
        out_shape=(shape, shape, shape, jax.ShapeDtypeStruct((288, 288), F32)),
        in_specs=vmem_specs(1),
        out_specs=tuple(vmem_specs(4)),
        scratch_shapes=[pltpu.VMEM((288, 3 * LANES), F32)],
        compiler_params=pltpu.CompilerParams(vmem_limit_bytes=LIMIT),
        name="spatial_unpack",
    )(received)


def flip(block):
    return pltpu.roll(block, HALF, 1)


def fold_tail(rest, r):
    return jnp.concatenate(
        [jnp.zeros((rest.shape[0], 32), F32), rest[:, 96 * r : 96 * r + 96]], axis=1
    )


def send_pack_kernel(me_ref, q_ref, k_ref, v_ref, g_ref, out0, out1, out2, out3, held):
    for part, ref in enumerate((q_ref, k_ref, v_ref)):
        rows = jnp.concatenate([ref[0], ref[1]], axis=0).astype(F32)
        columns = rows.T.astype(BF16)
        at = slice(part * LANES, (part + 1) * LANES)
        held[0, :, at] = columns[:288]
        held[1, :, at] = columns[288:576]
        held[2, :, at] = columns[576:864]
        held[3, :, at] = columns[864:]
    me = me_ref[0]
    grads = jnp.concatenate([g_ref[0], g_ref[1]], axis=0)
    for shift, out in enumerate((out0, out1, out2, out3)):
        out[:288] = held[lax.rem(me + shift, 4)]
        for third in range(3):
            out[288 + LANES * third : 288 + LANES * (third + 1)] = grads[
                :, 384 * third : 384 * (third + 1)
            ]


def send_pack(me, q, k, v, g):
    shape = jax.ShapeDtypeStruct((672, 3 * LANES), BF16)
    return pl.pallas_call(
        send_pack_kernel,
        out_shape=(shape,) * 4,
        in_specs=[pl.BlockSpec(memory_space=pltpu.SMEM)] + vmem_specs(4),
        out_specs=tuple(vmem_specs(4)),
        scratch_shapes=[pltpu.VMEM((4, 288, 3 * LANES), BF16)],
        compiler_params=pltpu.CompilerParams(vmem_limit_bytes=LIMIT),
        cost_estimate=LARGE,
        name="temporal_pack",
    )(me, q, k, v, g)


def piece_grads(ref):
    return jnp.concatenate(
        [ref[288 + LANES * third : 288 + LANES * (third + 1)] for third in range(3)], axis=1
    )


def rows_of(values):
    return jnp.concatenate([jnp.sum(value, axis=0, keepdims=True) for value in values], axis=0)


def frame_weights(query, keys):
    scores = rows_of([query * key for key in keys])
    peak = jnp.max(scores, axis=0, keepdims=True)
    raised = jnp.exp2((scores - peak) * (math.log2(math.e) / math.sqrt(HDIM)))
    return raised / jnp.sum(raised, axis=0, keepdims=True)


def rounded(value):
    return value.astype(BF16).astype(F32)


def head_rows(wide, head, part):
    rows = pl.ds(pl.multiple_of(head * HDIM, 8), HDIM)
    at = slice(part * LANES, (part + 1) * LANES)
    return [wide[shift, rows, at] for shift in range(4)]


def both_ways(blocks):
    out = []
    for block in blocks:
        out += [block, flip(block)]
    return out


def partial_kernel(me_ref, in0, in1, in2, in3, keep_ref, send_ref, wide, tout, full, *, scale):
    for shift, ref in enumerate((in0, in1, in2, in3)):
        wide[shift] = ref[:288].astype(F32)

    def body(head, _):
        queries = head_rows(wide, head, 0)
        keys = both_ways(head_rows(wide, head, 1))
        values = both_ways(head_rows(wide, head, 2))
        for shift in range(4):
            weights = rounded(frame_weights(queries[shift], keys))
            out = weights[0:1] * values[0]
            for j in range(1, 8):
                out = out + weights[j : j + 1] * values[j]
            tout[shift, pl.ds(pl.multiple_of(head * HDIM, 8), HDIM)] = out
        return 0

    lax.fori_loop(0, 4, body, 0)
    total = None
    for shift, ref in enumerate((in0, in1, in2, in3)):
        term = jnp.dot(tout[shift].astype(BF16), piece_grads(ref), preferred_element_type=F32)
        total = term if total is None else total + term
    total = total * scale
    full[0] = total[:144]
    full[1] = total[144:]
    core = me_ref[2]
    keep_ref[...] = full[core]
    send_ref[...] = full[1 - core].astype(BF16)


def weight_partial(me, pieces, scale):
    return pl.pallas_call(
        functools.partial(partial_kernel, scale=scale),
        out_shape=(
            jax.ShapeDtypeStruct((144, 1152), F32),
            jax.ShapeDtypeStruct((144, 1152), BF16),
        ),
        in_specs=[pl.BlockSpec(memory_space=pltpu.SMEM)] + vmem_specs(4),
        out_specs=tuple(vmem_specs(2)),
        scratch_shapes=[
            pltpu.VMEM((4, 288, 3 * LANES), F32),
            pltpu.VMEM((4, 288, LANES), F32),
            pltpu.VMEM((2, 144, 1152), F32),
        ],
        compiler_params=pltpu.CompilerParams(vmem_limit_bytes=LIMIT),
        cost_estimate=SMALL,
        name="weight_partial",
    )(me, *pieces)


def weight_split_kernel(keep_ref, got_ref, out_ref, full, part):
    full[...] = keep_ref[...] + got_ref[...].astype(F32)
    part[...] = jnp.zeros_like(part)
    row = lax.broadcasted_iota(jnp.int32, (16, 8, LANES), 1)
    for d in range(4):
        part[:, :288] = full[:, d * 288 : (d + 1) * 288]
        tiles = [
            part[:128, tile * LANES : (tile + 1) * LANES].reshape(16, 8, LANES)
            for tile in range(3)
        ]
        rest = part[128:144, :]
        for r in range(3):
            tiles[2] = tiles[2] + jnp.where(row == r, fold_tail(rest, r)[:, None, :], 0.0)
        out_ref[d * 16 : (d + 1) * 16] = jnp.concatenate(tiles, axis=1).astype(BF16)


def fold_tail(rest, r):
    return jnp.concatenate(
        [jnp.zeros((rest.shape[0], 32), F32), rest[:, 96 * r : 96 * r + 96]], axis=1
    )


def weight_split(keep, got):
    return pl.pallas_call(
        weight_split_kernel,
        out_shape=jax.ShapeDtypeStruct((64, 24, LANES), BF16),
        in_specs=vmem_specs(2),
        out_specs=pl.BlockSpec(memory_space=pltpu.VMEM),
        scratch_shapes=[pltpu.VMEM((144, 1152), F32), pltpu.VMEM((144, 3 * LANES), F32)],
        compiler_params=pltpu.CompilerParams(vmem_limit_bytes=LIMIT),
        cost_estimate=SMALL,
        name="weight_split",
    )(keep, got)


def unfold(block, full, start, last):
    for tile in range(3):
        at = slice(tile * LANES, (tile + 1) * LANES)
        full[start : start + 8, at] = block[tile * 8 : tile * 8 + 8]
    for r in range(3):
        full[last : last + 1, 96 * r : 96 * r + 96] = block[16 + r : 17 + r, 32:]


def weight_join_kernel(spatial_ref, in_ref, out_ref):
    total = in_ref[0].astype(F32)
    for s in range(1, 64):
        total = total + in_ref[s].astype(F32)
    copy = total.astype(BF16)
    for s in range(32):
        out_ref[s, : HDIM + FOLD] = spatial_ref[s]
        out_ref[s, HDIM + FOLD :] = copy


def weight_join(spatial, received):
    return pl.pallas_call(
        weight_join_kernel,
        out_shape=jax.ShapeDtypeStruct((32, HDIM + FOLD + 24, LANES), BF16),
        in_specs=vmem_specs(2),
        out_specs=pl.BlockSpec(memory_space=pltpu.VMEM),
        compiler_params=pltpu.CompilerParams(vmem_limit_bytes=LIMIT),
        cost_estimate=SMALL,
        name="weight_join",
    )(spatial, received)


def temporal_kernel(
    in0, in1, in2, in3, w_ref, out0, out1, out2, out3, wide, back, full
):
    for part in range(8):
        block = w_ref[part].astype(F32)
        for k, (start, end) in enumerate(CUTS):
            full[part * 144 + start : part * 144 + end] = block[
                : end - start, 288 * k : 288 * (k + 1)
            ]
    w = full[...].astype(BF16)
    for shift, ref in enumerate((in0, in1, in2, in3)):
        wide[shift, :, : 3 * LANES] = ref[:288].astype(F32)
        tgrad = rounded(jnp.dot(piece_grads(ref), w, preferred_element_type=F32))
        wide[shift, :, 3 * LANES :] = tgrad.T
    scale = 1.0 / math.sqrt(HDIM)

    def body(head, _):
        rows = pl.ds(pl.multiple_of(head * HDIM, 8), HDIM)
        queries = head_rows(wide, head, 0)
        keys = both_ways(head_rows(wide, head, 1))
        values = both_ways(head_rows(wide, head, 2))
        grads = head_rows(wide, head, 3)
        low_w, low_s = [], []
        for shift in range(4):
            weights = frame_weights(queries[shift], keys)
            pgrad = rows_of([grads[shift] * value for value in values])
            inner = jnp.sum(weights * pgrad, axis=0, keepdims=True)
            low_w.append(rounded(weights))
            low_s.append(rounded(weights * (pgrad - inner)))
            dq = low_s[shift][0:1] * keys[0]
            for j in range(1, 8):
                dq = dq + low_s[shift][j : j + 1] * keys[j]
            back[shift, rows, 0:LANES] = dq * scale
        for b in range(4):
            for part, (coefs, terms, factor) in enumerate(
                ((low_s, queries, scale), (low_w, grads, 1.0)), 1
            ):
                sums = []
                for way in range(2):
                    j = 2 * b + way
                    total = coefs[0][j : j + 1] * terms[0]
                    for shift in range(1, 4):
                        total = total + coefs[shift][j : j + 1] * terms[shift]
                    sums.append(total)
                back[b, rows, part * LANES : (part + 1) * LANES] = (
                    sums[0] + flip(sums[1])
                ) * factor
        return 0

    lax.fori_loop(0, 4, body, 0)
    for shift, out in enumerate((out0, out1, out2, out3)):
        out[...] = back[shift].astype(BF16)


def temporal_back(pieces, w):
    shape = jax.ShapeDtypeStruct((288, 3 * LANES), BF16)
    return pl.pallas_call(
        temporal_kernel,
        out_shape=(shape,) * 4,
        in_specs=vmem_specs(5),
        out_specs=tuple(vmem_specs(4)),
        scratch_shapes=[
            pltpu.VMEM((4, 288, 4 * LANES), F32),
            pltpu.VMEM((4, 288, 3 * LANES), F32),
            pltpu.VMEM((1152, 288), F32),
        ],
        compiler_params=pltpu.CompilerParams(vmem_limit_bytes=LIMIT),
        cost_estimate=LARGE,
        name="temporal_back",
    )(*pieces, w)


def receive_kernel(me_ref, in0, in1, in2, in3, dq_ref, dk_ref, dv_ref, held):
    me = me_ref[0]
    for shift, ref in enumerate((in0, in1, in2, in3)):
        held[lax.rem(me + shift, 4)] = ref[...]
    for part, out in enumerate((dq_ref, dk_ref, dv_ref)):
        at = slice(part * LANES, (part + 1) * LANES)
        columns = jnp.concatenate([held[t, :, at] for t in range(4)], axis=0).astype(F32)
        rows = columns.T.astype(BF16)
        out[0] = rows[:HALF]
        out[1] = rows[HALF:]


def receive(me, pieces):
    shape = jax.ShapeDtypeStruct((2, HALF, HEADS * HDIM), BF16)
    return pl.pallas_call(
        receive_kernel,
        out_shape=(shape,) * 3,
        in_specs=[pl.BlockSpec(memory_space=pltpu.SMEM)] + vmem_specs(4),
        out_specs=tuple(vmem_specs(3)),
        scratch_shapes=[pltpu.VMEM((4, 288, 3 * LANES), BF16)],
        compiler_params=pltpu.CompilerParams(vmem_limit_bytes=LIMIT),
        name="temporal_unpack",
    )(me, *pieces)


SWAP_CORE = [(0, 1), (1, 0)]
RING = [[(i, (i + s) % 4) for i in range(4)] for s in (1, 2, 3)]
RING_BACK = [[(i, (i - s) % 4) for i in range(4)] for s in (1, 2, 3)]


def shards(
    q_spatial,
    k_spatial,
    v_spatial,
    grad_spatial,
    q_temporal,
    k_temporal,
    v_temporal,
    grad_out,
    w_tout,
):
    core = lax.axis_index("c")
    me = jnp.stack([lax.axis_index("tm"), 4 * core + lax.axis_index("y"), core])
    space = ("z", "y", "c")
    packed, half = pack(
        me, q_spatial[0], k_spatial[0], v_spatial[0], grad_spatial[0], w_tout
    )
    weight = lax.all_gather(half, ("dp", "c"), axis=0, tiled=True).reshape(8, 64, 1152)
    packed, q, k, v, g = lax.optimization_barrier(
        (packed, q_temporal[0], k_temporal[0], v_temporal[0], grad_out[0])
    )
    received = lax.all_to_all(packed, space, split_axis=0, concat_axis=0, tiled=True)

    sends = send_pack(me, q, k, v, g)
    pieces = (sends[0],) + tuple(
        lax.ppermute(sends[shift], "tm", RING[shift - 1]) for shift in (1, 2, 3)
    )
    keep, send = weight_partial(me, pieces, 1.0 / math.sqrt(65536))
    blocks = weight_split(keep, lax.ppermute(send, "c", SWAP_CORE))

    received, blocks = lax.optimization_barrier((received, blocks))
    blocks = lax.all_to_all(blocks, ("dp", "z", "y"), split_axis=0, concat_axis=0, tiled=True)
    results = weight_join(attend(received), blocks)
    results, *pieces = lax.optimization_barrier((results,) + pieces)
    returned = lax.all_to_all(results, space, split_axis=0, concat_axis=0, tiled=True)

    backs = temporal_back(pieces, weight)
    homes = (backs[0],) + tuple(
        lax.ppermute(backs[shift], "tm", RING_BACK[shift - 1]) for shift in (1, 2, 3)
    )
    dq_t, dk_t, dv_t = receive(me, homes)
    dq, dk, dv, weight_grad = unpack(returned)
    return (dq[None], dk[None], dv[None], dq_t[None], dk_t[None], dv_t[None], weight_grad)


def solution(mesh):
    sizes = (mesh.shape["dp"], mesh.shape["tm"], 4, 4, 2)
    split = jax.sharding.Mesh(mesh.devices.reshape(sizes), ("dp", "tm", "z", "y", "c"))
    field = P("dp", "tm", ("z", "y", "c"), None)
    return jax.shard_map(
        shards,
        mesh=split,
        in_specs=(field,) * 8 + (P("dp", "tm"),),
        out_specs=(field,) * 6 + (P("dp", "tm"),),
        check_vma=False,
    )
```
